128 devices in a mesh: ctx: 8 (over y, core), tp: 16 (over x, z).
Axes of the slice: x: 4, y: 4, z: 4, core: 2. Of those that a mesh axis runs over, the one named last changes fastest.
Arguments:
- tokens: bfloat16 [4096, 5120], P(('ctx', 'tp')), may hold values from -6 to 6
- grad_out: bfloat16 [4096, 5120], P(('ctx', 'tp')), may hold values from -2 to 2
- gate_prob: bfloat16 [4096], P(('ctx', 'tp')), may hold values from 0.19921875 to 1
- expert_ids: int32 [4096, 1], P(('ctx', 'tp')), may hold values from 0 to 7; in each aligned block of 32 rows (0 to 31, 32 to 63, ...) at most 6 rows name the same one
- w_gate: bfloat16 [8, 5120, 6144], P('ctx', None, 'tp'), may hold values from -0.078125 to 0.078125
- w_up: bfloat16 [8, 5120, 6144], P('ctx', None, 'tp'), may hold values from -0.078125 to 0.078125
- w_down: bfloat16 [8, 6144, 5120], P('ctx', 'tp'), may hold values from -0.078125 to 0.078125
Outputs:
- grad_tokens: bfloat16 [4096, 5120], P(('ctx', 'tp'))
- grad_prob: bfloat16 [4096], P(('ctx', 'tp'))
- grad_gate: bfloat16 [8, 5120, 6144], P('ctx', None, 'tp')
- grad_up: bfloat16 [8, 5120, 6144], P('ctx', None, 'tp')
- grad_down: bfloat16 [8, 6144, 5120], P('ctx', 'tp')
The draws below stay inside these ranges and needn't reach their ends.
Inputs may be any that keep to these rules, and one draw needn't show every extreme that they name: `expert_ids`: among the 32 tokens of one device no expert is chosen by more than 6 tokens, and some expert is chosen by exactly 6; every expert is chosen somewhere.
All inputs are finite; a program needn't handle non-finite values.
Results may differ from the reference program's by a relative error of at most 0.0055.
Values may be sent and summed in bfloat16 or wider, within the bound.
A program may use at most 192 MiB of HBM per device.

```python
import math
import jax
import jax.numpy as jnp
import numpy as np
from jax import lax

D = 5120
FF = 6144
TOK_DEV = 32
EXPERTS = 8
CAP = 6
TOKENS = 4096
N_CTX = 8
N_TP = 16


def shard_levels(key, shape, cuts, least, top_value):
    def one(position, shards_of):
        heights = jax.random.uniform(jax.random.fold_in(jax.random.fold_in(key, 6), position), (shards_of,), jnp.float32, least / len(cuts), top_value / len(cuts))
        return jnp.repeat(jnp.exp(heights), shape[position] // shards_of).reshape((-1,) + (1,) * (len(shape) - position - 1))

    gain = one(*cuts[0])
    for cut in cuts[1:]:
        gain = gain * one(*cut)
    return gain


def deal_out(own_key, own, number, rows, count, top, bound, skew):
    order = jax.random.permutation(own_key, count)
    packed, usual = portions_of(count, rows * top, bound, skew, True), portions_of(count, rows * top, bound, skew, False)
    places = jnp.arange(count)

    def named(tallies, turn):
        used = int((tallies > 0).sum())
        fixed = max(1, used // 4)
        shifted = fixed + (places - fixed + turn * (used - fixed)) % max(1, count - fixed)
        return jnp.zeros((count,), jnp.int32).at[order[jnp.where(places < fixed, places, shifted)]].set(jnp.asarray(tallies, jnp.int32))

    tallies = jnp.where(number % 4 == 0, named(packed, number // 4), named(usual, number - number // 4 - 1))
    mixed = jax.random.permutation(jax.random.fold_in(own, 3), count)
    giver, taker = mixed[0:count // 2 * 2:2], mixed[1:count // 2 * 2:2]
    margin = jnp.minimum(tallies[giver] - 1, bound - tallies[taker]) // 2
    margin = jnp.where((giver == order[0]) | (taker == order[0]) | (tallies[taker] == 0), 0, jnp.maximum(margin, 0))
    shifted = jax.random.randint(jax.random.fold_in(own, 4), (count // 2,), 0, 1 << 20) % (margin + 1)
    tallies = tallies.at[giver].add(-shifted).at[taker].add(shifted)
    labels = jnp.searchsorted(jnp.cumsum(tallies), jnp.arange(rows * top), side="right").astype(jnp.int32)
    listing = labels.reshape(top, rows).T
    listing = listing[jax.random.permutation(jax.random.fold_in(own, 1), rows)]
    turn = jax.random.randint(jax.random.fold_in(own, 2), (rows, 1), 0, top)
    return jnp.take_along_axis(listing, (jnp.arange(top)[None, :] + turn) % top, axis=1)


def portions_of(amount, total, limit, slope, full):
    weights = [(1 << 20) // math.isqrt(rank ** slope) + 1 for rank in range(1, amount + 1)]
    largest = limit if full else min(limit, max(-(-total // amount), total * weights[0] // sum(weights)))
    least = 1 if total - largest >= amount - 1 else 0
    holding, surplus = [largest] + [least] * (amount - 1), total - largest - least * (amount - 1)
    while surplus > 0:
        movable = [i for i in range(1, amount) if holding[i] < largest] or [i for i in range(1, amount) if holding[i] < limit]
        mass, budget = sum([weights[i] for i in movable]), surplus
        for i in movable:
            addition = min(limit - holding[i], max(1, budget * weights[i] // mass), surplus)
            holding[i] = holding[i] + addition
            surplus = surplus - addition
    return np.array(holding)


def noise(stream_key, shape, spread, limit, cuts=(), kind=jnp.bfloat16):
    factor_of = shard_levels(stream_key, shape, cuts, -0.22, 0.18) if cuts else 1.0
    array = jax.random.normal(stream_key, shape, jnp.float32) * spread * factor_of
    return jnp.minimum(jnp.maximum(array, -limit), limit).astype(kind)


def setup_inputs(seed: int = 0) -> dict:
    key_list = jax.random.split(jax.random.key(seed), 8)
    tokens = noise(key_list[0], (TOKENS, D), 1.0, 6.0, ((0, 128),))
    grad_out = noise(key_list[1], (TOKENS, D), 0.3, 2.0, ((0, 128),))
    gate_prob = jnp.clip(0.19921875 + 0.80078125 * jax.random.uniform(key_list[2], (TOKENS,), jnp.float32) ** shard_levels(key_list[2], (TOKENS,), ((0, 128),), -0.2, 0.2), 0.19921875, 1.0).astype(jnp.bfloat16)
    expert_ids_keys = jax.random.split(jax.random.fold_in(key_list[3], 1), TOKENS // TOK_DEV)
    expert_ids_turns = jax.random.permutation(jax.random.fold_in(key_list[3], 3), TOKENS // TOK_DEV)
    expert_ids = jax.vmap(lambda own, number: deal_out(jax.random.fold_in(key_list[3], 2), own, number, TOK_DEV, EXPERTS, 1, CAP, 2))(expert_ids_keys, expert_ids_turns).reshape((TOKENS, 1))
    w_gate = noise(key_list[4], (EXPERTS, D, FF), D ** -0.5, 0.078125, ((0, 8), (2, 16)))
    w_up = noise(key_list[5], (EXPERTS, D, FF), D ** -0.5, 0.078125, ((0, 8), (2, 16)))
    w_down = noise(key_list[6], (EXPERTS, FF, D), FF ** -0.5, 0.078125, ((0, 8), (1, 16)))
    return dict(tokens=tokens, grad_out=grad_out, gate_prob=gate_prob, expert_ids=expert_ids, w_gate=w_gate, w_up=w_up, w_down=w_down)


def expert_grads(rows_in, rows_grad, prob, wg, wu, wd):
    g = jnp.dot(rows_in, wg, preferred_element_type=jnp.float32)
    u = jnp.dot(rows_in, wu, preferred_element_type=jnp.float32)
    sig = jax.nn.sigmoid(g)
    act = g * sig
    hidden = act * u
    probs = prob.astype(jnp.float32)[:, None]
    weighted = (probs * hidden).astype(jnp.bfloat16)
    dh_raw = lax.dot_general(rows_grad, wd, (((1,), (1,)), ((), ())), preferred_element_type=jnp.float32)
    prob_part = jnp.sum(hidden * dh_raw, axis=1)
    dh = probs * dh_raw
    dg = (dh * u * sig * (1.0 + g * (1.0 - sig))).astype(jnp.bfloat16)
    du = (dh * act).astype(jnp.bfloat16)
    grad_wd = lax.dot_general(weighted, rows_grad, (((0,), (0,)), ((), ())), preferred_element_type=jnp.float32).astype(jnp.bfloat16)
    grad_wg = lax.dot_general(rows_in, dg, (((0,), (0,)), ((), ())), preferred_element_type=jnp.float32).astype(jnp.bfloat16)
    grad_wu = lax.dot_general(rows_in, du, (((0,), (0,)), ((), ())), preferred_element_type=jnp.float32).astype(jnp.bfloat16)
    input_part = lax.dot_general(dg, wg, (((1,), (1,)), ((), ())), preferred_element_type=jnp.float32)
    input_part = input_part + lax.dot_general(du, wu, (((1,), (1,)), ((), ())), preferred_element_type=jnp.float32)
    return grad_wg, grad_wu, grad_wd, input_part, prob_part


def reference(tokens, grad_out, gate_prob, expert_ids, w_gate, w_up, w_down):
    devices = N_CTX * N_TP
    chosen = expert_ids[:, 0].astype(jnp.int32)
    onehot = (chosen.reshape(devices, TOK_DEV)[:, :, None] == jnp.arange(EXPERTS, dtype=jnp.int32)[None, None, :]).astype(jnp.int32)
    slots = jnp.sum((jnp.cumsum(onehot, axis=1) - 1) * onehot, axis=2).reshape(-1)
    source = jnp.arange(TOKENS, dtype=jnp.int32) // TOK_DEV
    place = (source * CAP + slots).astype(jnp.int32)
    index = jnp.full((EXPERTS, devices * CAP), TOKENS, jnp.int32).at[chosen, place].set(jnp.arange(TOKENS, dtype=jnp.int32))
    padded_in = jnp.concatenate([tokens, jnp.zeros((1, D), tokens.dtype)], axis=0)
    padded_grad = jnp.concatenate([grad_out, jnp.zeros((1, D), grad_out.dtype)], axis=0)
    padded_prob = jnp.concatenate([gate_prob, jnp.zeros((1,), gate_prob.dtype)], axis=0)

    def one_expert(expert):
        rows = index[expert]
        return expert_grads(padded_in[rows], padded_grad[rows], padded_prob[rows], w_gate[expert], w_up[expert], w_down[expert])

    grad_gate, grad_up, grad_down, input_part, prob_part = lax.map(one_expert, jnp.arange(EXPERTS, dtype=jnp.int32))
    flat = index.reshape(-1)
    grad_tokens = jnp.zeros((TOKENS + 1, D), jnp.float32).at[flat].add(input_part.reshape(-1, D))[:TOKENS].astype(jnp.bfloat16)
    grad_prob = jnp.zeros((TOKENS + 1,), jnp.float32).at[flat].add(prob_part.reshape(-1))[:TOKENS].astype(jnp.bfloat16)
    return grad_tokens, grad_prob, grad_gate, grad_up, grad_down
```

```python
import jax
import jax.numpy as jnp
from jax import lax
from jax.sharding import PartitionSpec as P


def dispatch_table(chosen, owners, capacity):
    onehot = (chosen[:, None] == jnp.arange(owners, dtype=jnp.int32)[None, :]).astype(jnp.int32)
    slots = jnp.sum((jnp.cumsum(onehot, axis=0) - 1) * onehot, axis=1)
    target = chosen * capacity + slots
    return (jnp.arange(owners * capacity, dtype=jnp.int32)[:, None] == target[None, :]).astype(
        jnp.bfloat16
    )


def expert_grads(rows_in, rows_grad, prob, wg, wu, wd):
    g = jnp.dot(rows_in, wg, preferred_element_type=jnp.float32)
    u = jnp.dot(rows_in, wu, preferred_element_type=jnp.float32)
    sig = jax.nn.sigmoid(g)
    act = g * sig
    hidden = act * u
    probs = prob.astype(jnp.float32)[:, None]
    weighted = (probs * hidden).astype(jnp.bfloat16)
    dh_raw = lax.dot_general(
        rows_grad, wd, (((1,), (1,)), ((), ())), preferred_element_type=jnp.float32
    )
    prob_part = jnp.sum(hidden * dh_raw, axis=1)
    dh = probs * dh_raw
    dg = (dh * u * sig * (1.0 + g * (1.0 - sig))).astype(jnp.bfloat16)
    du = (dh * act).astype(jnp.bfloat16)
    grad_wd = lax.dot_general(
        weighted, rows_grad, (((0,), (0,)), ((), ())), preferred_element_type=jnp.float32
    ).astype(jnp.bfloat16)
    grad_wg = lax.dot_general(
        rows_in, dg, (((0,), (0,)), ((), ())), preferred_element_type=jnp.float32
    ).astype(jnp.bfloat16)
    grad_wu = lax.dot_general(
        rows_in, du, (((0,), (0,)), ((), ())), preferred_element_type=jnp.float32
    ).astype(jnp.bfloat16)
    input_part = lax.dot_general(
        dg, wg, (((1,), (1,)), ((), ())), preferred_element_type=jnp.float32
    )
    input_part = input_part + lax.dot_general(
        du, wu, (((1,), (1,)), ((), ())), preferred_element_type=jnp.float32
    )
    return (grad_wg, grad_wu, grad_wd, input_part, prob_part)


def per_device(tokens, grad_out, gate_prob, expert_ids, w_gate, w_up, w_down):
    owners = lax.axis_size("ctx")
    groups = lax.axis_size("tp")
    count = tokens.shape[0]
    width = tokens.shape[1]
    capacity = 3 * count // (2 * owners)
    rows = owners * capacity
    table = dispatch_table(expert_ids[:, 0], owners, capacity)

    def route(values):
        return jnp.dot(table, values, preferred_element_type=jnp.float32).astype(jnp.bfloat16)

    send = jnp.concatenate(
        [route(tokens), route(grad_out), route(jnp.broadcast_to(gate_prob[:, None], (count, 128)))],
        axis=1,
    )
    plane = lax.all_to_all(
        send.reshape(owners, capacity, -1), "ctx", split_axis=0, concat_axis=0, tiled=True
    ).reshape(rows, -1)
    got = lax.all_gather(plane, "tp", axis=0, tiled=True)
    grad_wg, grad_wu, grad_wd, input_part, prob_part = expert_grads(
        got[:, :width],
        got[:, width : 2 * width],
        got[:, 2 * width],
        w_gate[0],
        w_up[0],
        w_down[0],
    )
    back_in = lax.psum_scatter(
        input_part.astype(jnp.bfloat16), "tp", scatter_dimension=0, tiled=True
    )
    back_prob = lax.psum_scatter(prob_part, "tp", scatter_dimension=0, tiled=True)
    final_in = lax.all_to_all(
        back_in.reshape(owners, capacity, width), "ctx", split_axis=0, concat_axis=0, tiled=True
    )
    final_prob = lax.all_to_all(
        back_prob.reshape(owners, capacity), "ctx", split_axis=0, concat_axis=0, tiled=True
    ).astype(jnp.bfloat16)
    grad_tokens = lax.dot_general(
        table,
        final_in.reshape(rows, width),
        (((0,), (0,)), ((), ())),
        preferred_element_type=jnp.float32,
    ).astype(jnp.bfloat16)
    grad_prob = lax.dot_general(
        table,
        final_prob.reshape(rows, 1),
        (((0,), (0,)), ((), ())),
        preferred_element_type=jnp.float32,
    )[:, 0].astype(jnp.bfloat16)
    return (grad_tokens, grad_prob, grad_wg[None], grad_wu[None], grad_wd[None])


def solution(mesh):
    in_specs = (
        P(("ctx", "tp"), None),
        P(("ctx", "tp"), None),
        P(("ctx", "tp")),
        P(("ctx", "tp"), None),
        P("ctx", None, "tp"),
        P("ctx", None, "tp"),
        P("ctx", "tp", None),
    )
    out_specs = (
        P(("ctx", "tp"), None),
        P(("ctx", "tp")),
        P("ctx", None, "tp"),
        P("ctx", None, "tp"),
        P("ctx", "tp", None),
    )
    return jax.shard_map(
        per_device, mesh=mesh, in_specs=in_specs, out_specs=out_specs, check_vma=False
    )
```

```python
import jax
import jax.numpy as jnp
from jax import lax
from jax.experimental import pallas as pl
from jax.experimental.pallas import tpu as pltpu
from jax.sharding import PartitionSpec as P

F32 = jnp.float32
BF16 = jnp.bfloat16
SIDE = 4
OWNERS = 8
PAIR = 2
CHUNKS = 3
CAPACITY = PAIR * CHUNKS
BLOCK = OWNERS * PAIR
ROWS = SIDE * SIDE * BLOCK
LANES = 128


def dot(a, b):
    return jnp.dot(a, b, preferred_element_type=F32)


def dot_nt(a, b):
    return lax.dot_general(a, b, (((1,), (1,)), ((), ())), preferred_element_type=F32)


def dot_tn(a, b):
    return lax.dot_general(a, b, (((0,), (0,)), ((), ())), preferred_element_type=F32)


def iota(shape, dim):
    return lax.broadcasted_iota(jnp.int32, shape, dim)


def select(mask):
    return jnp.where(mask, 1.0, 0.0).astype(BF16)


def kernel(
    tokens, grads, prob, ids, wg_in, wu_in, wd_in,
    out_tokens, out_prob, out_wg, out_wu, out_wd,
    wg, wu, wd, snd, rcv, ga, gb, part, s1, s2, t1, t2, fin, rsnd, rrcv,
    acc, dd, wei, pps, ppr,
    w_sem, o_sem, p1_send, p1_recv, ag_send, ag_recv, rs_send, rs_recv,
    pp_send, pp_recv, rt_send, rt_recv,
):
    count, width = tokens.shape
    units = wg.shape[1]
    quarter, eighth, half = width // 4, width // 8, width // 2
    c = lax.axis_index("ctx")
    t = lax.axis_index("tp")
    x, z = t // SIDE, t % SIDE

    def at_xz(xd, zd):
        return {"ctx": c, "tp": xd * SIDE + zd}

    def step(p, by):
        return (p + by + SIDE) % SIDE

    barrier = pltpu.get_barrier_semaphore()
    for dc in range(1, OWNERS):
        pl.semaphore_signal(
            barrier, inc=1, device_id={"ctx": (c + dc) % OWNERS, "tp": t},
            device_id_type=pl.DeviceIdType.MESH,
        )
    for d in range(1, SIDE * SIDE):
        pl.semaphore_signal(
            barrier, inc=1, device_id=at_xz(step(x, d // SIDE), step(z, d % SIDE)),
            device_id_type=pl.DeviceIdType.MESH,
        )

    loads = [
        pltpu.make_async_copy(src, dst, w_sem.at[i])
        for i, (src, dst) in enumerate(((wg_in.at[0], wg), (wu_in.at[0], wu), (wd_in.at[0], wd)))
    ]
    for copy in loads:
        copy.start()

    sent = []

    def send(src, dst, send_sem, recv_sem, device):
        copy = pltpu.make_async_remote_copy(
            src_ref=src, dst_ref=dst, send_sem=send_sem, recv_sem=recv_sem,
            device_id=device, device_id_type=pl.DeviceIdType.MESH,
        )
        copy.start()
        sent.append(copy)
        return copy

    onehot = jnp.where(ids[...] == iota((count, LANES), 1), 1.0, 0.0)
    lower = select(iota((count, count), 0) >= iota((count, count), 1))
    ranks = dot(lower, onehot.astype(BF16))
    slot = jnp.sum(ranks * onehot, axis=1, keepdims=True) - 1.0
    target = ids[...].astype(F32) * CAPACITY + slot
    eye = iota((count, count), 0) == iota((count, count), 1)
    target_row = jnp.sum(
        jnp.where(eye, jnp.broadcast_to(target, (count, count)), 0.0), axis=0, keepdims=True
    )
    prob_col = jnp.sum(
        jnp.where(eye, jnp.broadcast_to(prob[...].astype(F32), (count, count)), 0.0),
        axis=1, keepdims=True,
    )
    prob_wide = jnp.broadcast_to(prob_col, (count, LANES)).astype(BF16)
    slots = OWNERS * BLOCK

    def build(k):
        row = iota((slots, count), 0)
        inner = row % BLOCK
        want = (row // BLOCK) * CAPACITY + PAIR * k + inner % PAIR
        hit = jnp.broadcast_to(target_row, (slots, count)) == want.astype(F32)
        of_x = (inner // PAIR) % 2 == 0
        total = jnp.zeros((slots, quarter), F32)
        for q in range(4):
            mine = hit & (inner // 4 == q)
            cols = slice(q * quarter, (q + 1) * quarter)
            total += dot(select(mine & of_x), tokens[:, cols])
            total += dot(select(mine & ~of_x), grads[:, cols])
        snd[k, :, :, :quarter] = total.astype(BF16).reshape(OWNERS, BLOCK, quarter)
        probs = dot(select(hit & of_x & (inner // 4 == 0)), prob_wide)
        snd[k, :, :, quarter:] = probs.astype(BF16).reshape(OWNERS, BLOCK, LANES)

    p1 = {}

    def disperse(k):
        for dc in range(1, OWNERS):
            to = (c + dc) % OWNERS
            p1[k, dc] = send(
                snd.at[k, to], rcv.at[k, c], p1_send.at[k, dc], p1_recv.at[k, dc],
                {"ctx": to, "tp": t},
            )
        rcv[k, c] = snd[k, c]

    def assemble(k):
        for dc in range(1, OWNERS):
            p1[k, dc].wait_recv()
        row = iota((2 * BLOCK, slots), 0)
        col = iota((2 * BLOCK, slots), 1)
        one = row % BLOCK
        for q in range(4):
            where = (one // PAIR) * BLOCK + q * 4 + (row // BLOCK) * PAIR + one % PAIR
            pick = select(col == where)
            got = dot(pick, rcv[k, :, :, :quarter].reshape(slots, quarter)).astype(BF16)
            cols = slice(q * quarter, (q + 1) * quarter)
            ga[k, z, x, :, cols] = got[:BLOCK]
            gb[k, z, x, :, cols] = got[BLOCK:]
            if q == 0:
                probs = dot(pick, rcv[k, :, :, quarter:].reshape(slots, LANES)).astype(BF16)
                ga[k, z, x, :, width:] = probs[:BLOCK]

    ag = {}
    halves = (
        (pl.ds(0, half), pl.ds(half, half + LANES)),
        (pl.ds(0, half), pl.ds(half, half)),
    )

    def ag_send_one(k, arr, n, ref, device):
        ag[k, arr, n] = send(ref, ref, ag_send.at[k, arr, n], ag_recv.at[k, arr, n], device)

    def near(arr, stage, by):
        along_x = (arr == 0) == (stage == 1)
        return at_xz(step(x, by), z) if along_x else at_xz(x, step(z, by))

    def single(k, arr, by, cols=None):
        buf = (ga, gb)[arr]
        xd, zd = (step(x, by), z) if arr == 0 else (x, step(z, by))
        return buf.at[k, zd, xd] if cols is None else buf.at[k, zd, xd, :, cols]

    def slab(k, arr, by, cols=None):
        if arr == 0:
            zd = step(z, by)
            return ga.at[k, zd] if cols is None else ga.at[k, zd, :, :, cols]
        xd = step(x, by)
        return gb.at[k, :, xd] if cols is None else gb.at[k, :, xd, :, cols]

    def g1(k):
        for arr in range(2):
            ag_send_one(k, arr, 0, single(k, arr, 0), near(arr, 1, 1))
            ag_send_one(k, arr, 1, single(k, arr, 0), near(arr, 1, -1))

    def g2(k):
        for arr in range(2):
            ag[k, arr, 0].wait_recv()
            ag_send_one(k, arr, 2, single(k, arr, -1, halves[arr][0]), near(arr, 1, 1))
            ag[k, arr, 1].wait_recv()
            ag_send_one(k, arr, 3, single(k, arr, 1, halves[arr][1]), near(arr, 1, -1))

    def g3(k):
        for arr in range(2):
            ag[k, arr, 2].wait_recv()
            ag[k, arr, 3].wait_recv()
            ag_send_one(k, arr, 4, slab(k, arr, 0), near(arr, 2, 1))
            ag_send_one(k, arr, 5, slab(k, arr, 0), near(arr, 2, -1))

    def g4(k):
        for arr in range(2):
            ag[k, arr, 4].wait_recv()
            ag_send_one(k, arr, 6, slab(k, arr, -1, halves[arr][0]), near(arr, 2, 1))
        for arr in range(2):
            ag[k, arr, 5].wait_recv()
            ag_send_one(k, arr, 7, slab(k, arr, 1, halves[arr][1]), near(arr, 2, -1))

    def g5(k):
        for arr in range(2):
            ag[k, arr, 6].wait_recv()
            ag[k, arr, 7].wait_recv()

    deep = quarter
    wide = width // 10

    def forward(k):
        def products(i, first):
            at = pl.ds(pl.multiple_of(i * deep, deep), deep)
            rows_in = ga[k, :, :, :, at].reshape(ROWS, deep)
            rows_grad = gb[k, :, :, :, at].reshape(ROWS, deep)
            for n, value in enumerate((
                lambda: dot(rows_in, wg[at, :]),
                lambda: dot(rows_in, wu[at, :]),
                lambda: dot_nt(rows_grad, wd[:, at]),
            )):
                acc[n] = value() if first else acc[n] + value()

        products(0, True)

        @pl.loop(1, width // deep)
        def _(i):
            products(i, False)

        part_rows = 2 * LANES // 4

        @pl.loop(0, ROWS // part_rows)
        def _(i):
            at = pl.ds(pl.multiple_of(i * part_rows, part_rows), part_rows)
            keep = pl.ds(pl.multiple_of(k * ROWS + i * part_rows, part_rows), part_rows)
            g, u, raw = acc[0, at, :], acc[1, at, :], acc[2, at, :]
            sig = jax.nn.sigmoid(g)
            act = g * sig
            hidden = act * u
            probs = ga[k, i, :, :, width:].reshape(part_rows, LANES).astype(F32)[:, :1]
            wei[keep, :] = (probs * hidden).astype(BF16)
            dh = probs * raw
            dd[keep, :units] = (dh * u * sig * (1.0 + g * (1.0 - sig))).astype(BF16)
            dd[keep, units:] = (dh * act).astype(BF16)
            sums = jnp.broadcast_to(
                jnp.sum(hidden * raw, axis=1, keepdims=True), (part_rows, LANES)
            )
            spot = iota((part_rows, LANES), 1) == k * BLOCK + iota((part_rows, LANES), 0) % BLOCK
            lanes = jnp.sum(
                jnp.where(spot, sums, 0.0).reshape(SIDE, BLOCK, LANES), axis=1, keepdims=True
            )
            lanes = jnp.broadcast_to(lanes, (SIDE, 8, LANES))
            pps[i] = lanes if k == 0 else pps[i] + lanes

    def backward(k):
        dg = dd[k * ROWS:(k + 1) * ROWS, :units]
        du = dd[k * ROWS:(k + 1) * ROWS, units:]

        @pl.loop(0, width // wide)
        def _(i):
            at = pl.ds(pl.multiple_of(i * wide, wide), wide)
            value = dot_nt(dg, wg[at, :]) + dot_nt(du, wu[at, :])
            part[k, :, :, :, at] = value.astype(BF16).reshape(SIDE, SIDE, BLOCK, wide)

    rs = {}

    def rs_send_one(k, h, n, src, dst, device):
        rs[k, h, n] = send(src, dst, rs_send.at[k, h, n], rs_recv.at[k, h, n], device)

    def cols_of(h, piece):
        if piece is None:
            return slice(h * half, (h + 1) * half)
        return slice(h * half + piece * quarter, h * half + (piece + 1) * quarter)

    def group(h, by):
        return (step(z, by), slice(None)) if h == 0 else (slice(None), step(x, by))

    def own(h, by):
        return (z, step(x, by)) if h == 0 else (step(z, by), x)

    def add_into(where, others):
        value = part[where].astype(F32)
        for other in others:
            value += other[...].astype(F32)
        part[where] = value.astype(BF16)

    def r1(k):
        for h in range(2):
            far = group(h, 2)
            rs_send_one(k, h, 0, part.at[(k,) + far + (slice(None), cols_of(h, 0))],
                        s1.at[k, h, 0], near(h, 2, 1))
            rs_send_one(k, h, 1, part.at[(k,) + far + (slice(None), cols_of(h, 1))],
                        s1.at[k, h, 1], near(h, 2, -1))

    def r2(k):
        for h in range(2):
            for side, by in ((0, 1), (1, -1)):
                rs[k, h, side].wait_recv()
                to = (k,) + group(h, by) + (slice(None),)
                add_into(to + (cols_of(h, side),), (s1.at[k, h, side],))
                rs_send_one(k, h, 2 + side, part.at[to + (cols_of(h, None),)],
                            s2.at[k, h, side], near(h, 2, by))

    def r3(k):
        for h in range(2):
            rs[k, h, 2].wait_recv()
            rs[k, h, 3].wait_recv()
            far = (k,) + own(h, 2) + (slice(None),)
            mine = (k,) + group(h, 0) + (slice(None), cols_of(h, None))
            add_into(mine, (s2.at[k, h, 0], s2.at[k, h, 1]))
            rs_send_one(k, h, 4, part.at[far + (cols_of(h, 0),)], t1.at[k, h, 0], near(h, 1, 1))
            rs_send_one(k, h, 5, part.at[far + (cols_of(h, 1),)], t1.at[k, h, 1], near(h, 1, -1))

    def r4(k):
        for h in range(2):
            for side, by in ((0, 1), (1, -1)):
                rs[k, h, 4 + side].wait_recv()
                to = (k,) + own(h, by) + (slice(None),)
                add_into(to + (cols_of(h, side),), (t1.at[k, h, side],))
                rs_send_one(k, h, 6 + side, part.at[to + (cols_of(h, None),)],
                            t2.at[k, h, side], near(h, 1, by))

    rt = {}

    def r5(k):
        for h in range(2):
            rs[k, h, 6].wait_recv()
            rs[k, h, 7].wait_recv()
            value = part[(k, z, x, slice(None), cols_of(h, None))].astype(F32)
            value += t2[k, h, 0].astype(F32) + t2[k, h, 1].astype(F32)
            fin[:, cols_of(h, None)] = value.astype(BF16)
        row = iota((slots, BLOCK), 0)
        inner = row % BLOCK
        home = iota((slots, BLOCK), 1) == (row // BLOCK) * PAIR + inner % PAIR
        total = jnp.zeros((slots, eighth), F32)
        for q in range(8):
            total += dot(select(home & (inner // PAIR == q)), fin[:, q * eighth:(q + 1) * eighth])
        rsnd[k, :, :, :eighth] = total.astype(BF16).reshape(OWNERS, BLOCK, eighth)
        span = pl.ds(0, eighth)
        if k == CHUNKS - 1:
            span = pl.ds(0, eighth + LANES)
            for d in range(1, SIDE * SIDE):
                pp[d].wait_recv()
            ppr[0] = pps[z, x]
            summed = jnp.sum(ppr[...], axis=0)[:1]
            held = CHUNKS * BLOCK
            diagonal = iota((held, LANES), 0) == iota((held, LANES), 1)
            column = jnp.sum(
                jnp.where(diagonal, jnp.broadcast_to(summed, (held, LANES)), 0.0),
                axis=1, keepdims=True,
            )
            column = jnp.broadcast_to(column, (held, LANES)).astype(BF16)
            row = iota((slots, held), 0)
            inner = row % BLOCK
            place = (inner // PAIR) * BLOCK + (row // BLOCK) * PAIR + inner % PAIR
            probs = dot(select(iota((slots, held), 1) == place), column)
            rsnd[k, :, :, eighth:] = probs.astype(BF16).reshape(OWNERS, BLOCK, LANES)
        for dc in range(1, OWNERS):
            to = (c + dc) % OWNERS
            rt[k, dc] = send(
                rsnd.at[k, to, :, span], rrcv.at[k, c, :, span],
                rt_send.at[k, dc], rt_recv.at[k, dc], {"ctx": to, "tp": t},
            )
        rrcv[k, c] = rsnd[k, c]

    pp = {}

    def probs_out():
        for d in range(1, SIDE * SIDE):
            xd, zd = step(x, d // SIDE), step(z, d % SIDE)
            pp[d] = send(pps.at[zd, xd], ppr.at[d], pp_send.at[d], pp_recv.at[d], at_xz(xd, zd))

    def weight_in(first, last):
        @pl.loop(first, last)
        def _(i):
            at = pl.ds(pl.multiple_of(i * wide, wide), wide)
            rows_in = ga[:, :, :, :, at].reshape(CHUNKS * ROWS, wide)
            value = dot_tn(rows_in, dd[...])
            wg[at, :] = value[:, :units].astype(BF16)
            wu[at, :] = value[:, units:].astype(BF16)

    def weight_down():
        @pl.loop(0, width // wide)
        def _(i):
            at = pl.ds(pl.multiple_of(i * wide, wide), wide)
            rows_grad = gb[:, :, :, :, at].reshape(CHUNKS * ROWS, wide)
            wd[:, at] = dot_tn(wei[...], rows_grad).astype(BF16)

    stores = [
        pltpu.make_async_copy(src, dst, o_sem.at[i])
        for i, (src, dst) in enumerate(
            ((wg, out_wg.at[0]), (wu, out_wu.at[0]), (wd, out_wd.at[0]))
        )
    ]

    build(0)
    pl.semaphore_wait(barrier, OWNERS - 1 + SIDE * SIDE - 1)
    disperse(0)
    build(1)
    disperse(1)
    build(2)
    disperse(2)
    assemble(0)
    g1(0)
    assemble(1)
    g1(1)
    g2(0)
    assemble(2)
    g1(2)
    g3(0)
    g2(1)
    g3(1)
    g2(2)
    g4(0)
    g3(2)
    for copy in loads:
        copy.wait()
    g5(0)
    forward(0)
    backward(0)
    r1(0)
    g4(1)
    r2(0)
    g5(1)
    g4(2)
    forward(1)
    backward(1)
    r1(1)
    r3(0)
    r2(1)
    r4(0)
    g5(2)
    forward(2)
    backward(2)
    r1(2)
    probs_out()
    r3(1)
    r5(0)
    weight_in(0, 3)
    r2(2)
    r4(1)
    weight_in(3, 6)
    r3(2)
    r5(1)
    weight_in(6, 8)
    r4(2)
    weight_in(8, 10)
    stores[0].start()
    stores[1].start()
    r5(2)
    weight_down()
    stores[2].start()

    for k in range(CHUNKS):
        for dc in range(1, OWNERS):
            rt[k, dc].wait_recv()
    row = iota((count, slots), 1)
    inner = row % BLOCK
    base = (row // BLOCK) * CAPACITY + inner % PAIR
    hits = [
        jnp.broadcast_to(target, (count, slots)) == (base + PAIR * k).astype(F32)
        for k in range(CHUNKS)
    ]
    for q in range(8):
        total = jnp.zeros((count, eighth), F32)
        for k in range(CHUNKS):
            total += dot(
                select(hits[k] & (inner // PAIR == q)),
                rrcv[k, :, :, :eighth].reshape(slots, eighth),
            )
        out_tokens[:, q * eighth:(q + 1) * eighth] = total.astype(BF16)
    total = jnp.zeros((count, LANES), F32)
    for k in range(CHUNKS):
        total += dot(
            select(hits[k] & (inner // PAIR == k)),
            rrcv[CHUNKS - 1, :, :, eighth:].reshape(slots, LANES),
        )
    out_prob[...] = total.astype(BF16)

    for copy in sent:
        copy.wait_send()
    for copy in stores:
        copy.wait()


def per_device(tokens, grad_out, gate_prob, expert_ids, w_gate, w_up, w_down):
    count, width = tokens.shape
    units = w_gate.shape[2]
    quarter, eighth, half = width // 4, width // 8, width // 2
    vmem = pl.BlockSpec(memory_space=pltpu.VMEM)
    anywhere = pl.BlockSpec(memory_space=pl.ANY)
    rows = CHUNKS * ROWS
    dma = pltpu.SemaphoreType.DMA
    grad_tokens, grad_prob, grad_wg, grad_wu, grad_wd = pl.pallas_call(
        kernel,
        out_shape=(
            jax.ShapeDtypeStruct((count, width), BF16),
            jax.ShapeDtypeStruct((count, LANES), BF16),
            jax.ShapeDtypeStruct(w_gate.shape, BF16),
            jax.ShapeDtypeStruct(w_up.shape, BF16),
            jax.ShapeDtypeStruct(w_down.shape, BF16),
        ),
        in_specs=[vmem] * 4 + [anywhere] * 3,
        out_specs=[vmem] * 2 + [anywhere] * 3,
        scratch_shapes=[
            pltpu.VMEM((width, units), BF16),
            pltpu.VMEM((width, units), BF16),
            pltpu.VMEM((units, width), BF16),
            pltpu.VMEM((CHUNKS, OWNERS, BLOCK, quarter + LANES), BF16),
            pltpu.VMEM((CHUNKS, OWNERS, BLOCK, quarter + LANES), BF16),
            pltpu.VMEM((CHUNKS, SIDE, SIDE, BLOCK, width + LANES), BF16),
            pltpu.VMEM((CHUNKS, SIDE, SIDE, BLOCK, width), BF16),
            pltpu.VMEM((CHUNKS, SIDE, SIDE, BLOCK, width), BF16),
            pltpu.VMEM((CHUNKS, 2, 2, SIDE, BLOCK, quarter), BF16),
            pltpu.VMEM((CHUNKS, 2, 2, SIDE, BLOCK, half), BF16),
            pltpu.VMEM((CHUNKS, 2, 2, BLOCK, quarter), BF16),
            pltpu.VMEM((CHUNKS, 2, 2, BLOCK, half), BF16),
            pltpu.VMEM((BLOCK, width), BF16),
            pltpu.VMEM((CHUNKS, OWNERS, BLOCK, eighth + LANES), BF16),
            pltpu.VMEM((CHUNKS, OWNERS, BLOCK, eighth + LANES), BF16),
            pltpu.VMEM((3, ROWS, units), F32),
            pltpu.VMEM((rows, 2 * units), BF16),
            pltpu.VMEM((rows, units), BF16),
            pltpu.VMEM((SIDE, SIDE, 8, LANES), F32),
            pltpu.VMEM((SIDE * SIDE, 8, LANES), F32),
            dma((3,)),
            dma((3,)),
            dma((CHUNKS, OWNERS)),
            dma((CHUNKS, OWNERS)),
            dma((CHUNKS, 2, 8)),
            dma((CHUNKS, 2, 8)),
            dma((CHUNKS, 2, 8)),
            dma((CHUNKS, 2, 8)),
            dma((SIDE * SIDE,)),
            dma((SIDE * SIDE,)),
            dma((CHUNKS, OWNERS)),
            dma((CHUNKS, OWNERS)),
        ],
        compiler_params=pltpu.CompilerParams(
            collective_id=0, has_side_effects=True, vmem_limit_bytes=60 * 2**20
        ),
    )(tokens, grad_out, gate_prob[None], expert_ids, w_gate, w_up, w_down)
    return grad_tokens, grad_prob[:, 0], grad_wg, grad_wu, grad_wd


def solution(mesh):
    in_specs = (
        P(("ctx", "tp"), None),
        P(("ctx", "tp"), None),
        P(("ctx", "tp")),
        P(("ctx", "tp"), None),
        P("ctx", None, "tp"),
        P("ctx", None, "tp"),
        P("ctx", "tp", None),
    )
    out_specs = (
        P(("ctx", "tp"), None),
        P(("ctx", "tp")),
        P("ctx", None, "tp"),
        P("ctx", None, "tp"),
        P("ctx", "tp", None),
    )
    return jax.shard_map(
        per_device, mesh=mesh, in_specs=in_specs, out_specs=out_specs, check_vma=False
    )
```

```python
import jax
import jax.numpy as jnp
from jax import lax
from jax.experimental import pallas as pl
from jax.experimental.pallas import tpu as pltpu
from jax.sharding import PartitionSpec as P

F32 = jnp.float32
BF16 = jnp.bfloat16
SIDE = 4
OWNERS = 8
PAIR = 2
CHUNKS = 3
CAPACITY = PAIR * CHUNKS
BLOCK = OWNERS * PAIR
ROWS = SIDE * SIDE * BLOCK
LANES = 128


def dot(a, b):
    return jnp.dot(a, b, preferred_element_type=F32)


def dot_nt(a, b):
    return lax.dot_general(a, b, (((1,), (1,)), ((), ())), preferred_element_type=F32)


def dot_tn(a, b):
    return lax.dot_general(a, b, (((0,), (0,)), ((), ())), preferred_element_type=F32)


def iota(shape, dim):
    return lax.broadcasted_iota(jnp.int32, shape, dim)


def select(mask):
    return jnp.where(mask, 1.0, 0.0).astype(BF16)


def kernel(
    tokens, grads, prob, ids, wg_in, wu_in, wd_in,
    out_tokens, out_prob, out_wg, out_wu, out_wd,
    stk, snd, rcv, ga, gb, part, s1, s2, t1, t2, fin, rsnd, rrcv,
    acc, dd, wei, pps, ppr,
    i_sem, w_sem, p1_send, p1_recv, ag_send, ag_recv, rs_send, rs_recv,
    pp_send, pp_recv, rt_send, rt_recv,
):
    count, width = tokens.shape
    wg, wu, wd = out_wg.at[0], out_wu.at[0], out_wd.at[0]
    units = wg.shape[1]
    quarter, eighth, half = width // 4, width // 8, width // 2
    c = lax.axis_index("ctx")
    t = lax.axis_index("tp")
    x, z = t // SIDE, t % SIDE

    def at_xz(xd, zd):
        return {"ctx": c, "tp": xd * SIDE + zd}

    def step(p, by):
        return (p + by + SIDE) % SIDE

    barrier = pltpu.get_barrier_semaphore()
    for dc in range(1, OWNERS):
        pl.semaphore_signal(
            barrier, inc=1, device_id={"ctx": (c + dc) % OWNERS, "tp": t},
            device_id_type=pl.DeviceIdType.MESH,
        )
    for d in range(1, SIDE * SIDE):
        pl.semaphore_signal(
            barrier, inc=1, device_id=at_xz(step(x, d // SIDE), step(z, d % SIDE)),
            device_id_type=pl.DeviceIdType.MESH,
        )

    stacking = [
        pltpu.make_async_copy(
            src.at[:, q * quarter:(q + 1) * quarter],
            stk.at[pl.ds((2 * q + n) * count, count), pl.ds(0, quarter)],
            i_sem.at[2 * q + n],
        )
        for q in range(4)
        for n, src in enumerate((tokens, grads))
    ]
    for copy in stacking:
        copy.start()
    loads = [
        pltpu.make_async_copy(src, dst, w_sem.at[i])
        for i, (src, dst) in enumerate(((wg_in.at[0], wg), (wu_in.at[0], wu), (wd_in.at[0], wd)))
    ]
    for copy in loads:
        copy.start()

    sent = []

    def send(src, dst, send_sem, recv_sem, device):
        copy = pltpu.make_async_remote_copy(
            src_ref=src, dst_ref=dst, send_sem=send_sem, recv_sem=recv_sem,
            device_id=device, device_id_type=pl.DeviceIdType.MESH,
        )
        copy.start()
        sent.append(copy)
        return copy

    deck = 8 * count

    def column(line):
        eye = iota((count, count), 0) == iota((count, count), 1)
        spread = jnp.broadcast_to(line[...].astype(F32), (count, count))
        return jnp.sum(jnp.where(eye, spread, 0.0), axis=1, keepdims=True)

    chosen = column(ids)
    onehot = jnp.where(chosen == iota((count, LANES), 1).astype(F32), 1.0, 0.0)
    lower = select(iota((count, count), 0) >= iota((count, count), 1))
    ranks = dot(lower, onehot.astype(BF16))
    slot = jnp.sum(ranks * onehot, axis=1, keepdims=True) - 1.0
    target = chosen * CAPACITY + slot
    target_row = jnp.sum(
        jnp.where(
            iota((count, deck), 0) == iota((count, deck), 1) % count,
            jnp.broadcast_to(target, (count, deck)), 0.0,
        ),
        axis=0, keepdims=True,
    )
    stk[:, quarter:] = jnp.zeros((deck, LANES), BF16)
    stk[:count, quarter:] = jnp.broadcast_to(column(prob), (count, LANES)).astype(BF16)
    slots = OWNERS * BLOCK

    def build(k):
        row, col = iota((slots, deck), 0), iota((slots, deck), 1)
        inner = row % BLOCK
        want = (row // BLOCK) * CAPACITY + PAIR * k + inner % PAIR
        hit = jnp.broadcast_to(target_row, (slots, deck)) == want.astype(F32)
        pick = select(hit & (inner // PAIR == col // count))
        snd[k] = dot(pick, stk[...]).astype(BF16).reshape(OWNERS, BLOCK, quarter + LANES)

    p1 = {}

    def disperse(k):
        for dc in range(1, OWNERS):
            to = (c + dc) % OWNERS
            p1[k, dc] = send(
                snd.at[k, to], rcv.at[k, c], p1_send.at[k, dc], p1_recv.at[k, dc],
                {"ctx": to, "tp": t},
            )
        rcv[k, c] = snd[k, c]

    def assemble(k):
        for dc in range(1, OWNERS):
            p1[k, dc].wait_recv()
        row, col = iota((slots, slots), 0), iota((slots, slots), 1)
        one = row % BLOCK
        where = (one // PAIR) * BLOCK + (row // BLOCK) * PAIR + one % PAIR
        got = dot(select(col == where), rcv[k].reshape(slots, quarter + LANES)).astype(BF16)
        for q in range(4):
            cols = slice(q * quarter, (q + 1) * quarter)
            ga[k, z, x, :, cols] = got[2 * q * BLOCK:(2 * q + 1) * BLOCK, :quarter]
            gb[k, z, x, :, cols] = got[(2 * q + 1) * BLOCK:(2 * q + 2) * BLOCK, :quarter]
        ga[k, z, x, :, width:] = got[:BLOCK, quarter:]

    ag = {}
    halves = (
        (pl.ds(0, half), pl.ds(half, half + LANES)),
        (pl.ds(0, half), pl.ds(half, half)),
    )

    def ag_send_one(k, arr, n, ref, device):
        ag[k, arr, n] = send(ref, ref, ag_send.at[k, arr, n], ag_recv.at[k, arr, n], device)

    def near(arr, stage, by):
        along_x = (arr == 0) == (stage == 1)
        return at_xz(step(x, by), z) if along_x else at_xz(x, step(z, by))

    def single(k, arr, by, cols=None):
        buf = (ga, gb)[arr]
        xd, zd = (step(x, by), z) if arr == 0 else (x, step(z, by))
        return buf.at[k, zd, xd] if cols is None else buf.at[k, zd, xd, :, cols]

    def slab(k, arr, by, cols=None):
        if arr == 0:
            zd = step(z, by)
            return ga.at[k, zd] if cols is None else ga.at[k, zd, :, :, cols]
        xd = step(x, by)
        return gb.at[k, :, xd] if cols is None else gb.at[k, :, xd, :, cols]

    def g1(k):
        for arr in range(2):
            ag_send_one(k, arr, 0, single(k, arr, 0), near(arr, 1, 1))
            ag_send_one(k, arr, 1, single(k, arr, 0), near(arr, 1, -1))

    def g2(k):
        for arr in range(2):
            ag[k, arr, 0].wait_recv()
            ag_send_one(k, arr, 2, single(k, arr, -1, halves[arr][0]), near(arr, 1, 1))
            ag[k, arr, 1].wait_recv()
            ag_send_one(k, arr, 3, single(k, arr, 1, halves[arr][1]), near(arr, 1, -1))

    def g3(k):
        for arr in range(2):
            ag[k, arr, 2].wait_recv()
            ag[k, arr, 3].wait_recv()
            ag_send_one(k, arr, 4, slab(k, arr, 0), near(arr, 2, 1))
            ag_send_one(k, arr, 5, slab(k, arr, 0), near(arr, 2, -1))

    def g4(k):
        for arr in range(2):
            ag[k, arr, 4].wait_recv()
            ag_send_one(k, arr, 6, slab(k, arr, -1, halves[arr][0]), near(arr, 2, 1))
        for arr in range(2):
            ag[k, arr, 5].wait_recv()
            ag_send_one(k, arr, 7, slab(k, arr, 1, halves[arr][1]), near(arr, 2, -1))

    def g5(k):
        for arr in range(2):
            ag[k, arr, 6].wait_recv()
            ag[k, arr, 7].wait_recv()

    deep = quarter
    wide = width // 10

    def forward(k):
        def products(i, first):
            at = pl.ds(pl.multiple_of(i * deep, deep), deep)
            rows_in = ga[k, :, :, :, at].reshape(ROWS, deep)
            rows_grad = gb[k, :, :, :, at].reshape(ROWS, deep)
            for n, value in enumerate((
                lambda: dot(rows_in, wg[at, :]),
                lambda: dot(rows_in, wu[at, :]),
                lambda: dot_nt(rows_grad, wd[:, at]),
            )):
                acc[n] = value() if first else acc[n] + value()

        products(0, True)

        @pl.loop(1, width // deep)
        def _(i):
            products(i, False)

        part_rows = 2 * LANES // 4

        @pl.loop(0, ROWS // part_rows)
        def _(i):
            at = pl.ds(pl.multiple_of(i * part_rows, part_rows), part_rows)
            keep = pl.ds(pl.multiple_of(k * ROWS + i * part_rows, part_rows), part_rows)
            g, u, raw = acc[0, at, :], acc[1, at, :], acc[2, at, :]
            sig = jax.nn.sigmoid(g)
            act = g * sig
            hidden = act * u
            probs = ga[k, i, :, :, width:].reshape(part_rows, LANES).astype(F32)[:, :1]
            wei[keep, :] = (probs * hidden).astype(BF16)
            dh = probs * raw
            dd[keep, :units] = (dh * u * sig * (1.0 + g * (1.0 - sig))).astype(BF16)
            dd[keep, units:] = (dh * act).astype(BF16)
            sums = jnp.broadcast_to(
                jnp.sum(hidden * raw, axis=1, keepdims=True), (part_rows, LANES)
            )
            spot = iota((part_rows, LANES), 1) == k * BLOCK + iota((part_rows, LANES), 0) % BLOCK
            lanes = jnp.sum(
                jnp.where(spot, sums, 0.0).reshape(SIDE, BLOCK, LANES), axis=1, keepdims=True
            )
            lanes = jnp.broadcast_to(lanes, (SIDE, 8, LANES))
            pps[i] = lanes if k == 0 else pps[i] + lanes

    def backward(k):
        dg = dd[k * ROWS:(k + 1) * ROWS, :units]
        du = dd[k * ROWS:(k + 1) * ROWS, units:]

        @pl.loop(0, width // wide)
        def _(i):
            at = pl.ds(pl.multiple_of(i * wide, wide), wide)
            value = dot_nt(dg, wg[at, :]) + dot_nt(du, wu[at, :])
            part[k, :, :, :, at] = value.astype(BF16).reshape(SIDE, SIDE, BLOCK, wide)

    rs = {}

    def rs_send_one(k, h, n, src, dst, device):
        rs[k, h, n] = send(src, dst, rs_send.at[k, h, n], rs_recv.at[k, h, n], device)

    def cols_of(h, piece):
        if piece is None:
            return slice(h * half, (h + 1) * half)
        return slice(h * half + piece * quarter, h * half + (piece + 1) * quarter)

    def group(h, by):
        return (step(z, by), slice(None)) if h == 0 else (slice(None), step(x, by))

    def own(h, by):
        return (z, step(x, by)) if h == 0 else (step(z, by), x)

    def add_into(where, others):
        value = part[where].astype(F32)
        for other in others:
            value += other[...].astype(F32)
        part[where] = value.astype(BF16)

    def r1(k):
        for h in range(2):
            far = group(h, 2)
            rs_send_one(k, h, 0, part.at[(k,) + far + (slice(None), cols_of(h, 0))],
                        s1.at[k, h, 0], near(h, 2, 1))
            rs_send_one(k, h, 1, part.at[(k,) + far + (slice(None), cols_of(h, 1))],
                        s1.at[k, h, 1], near(h, 2, -1))

    def r2(k):
        for h in range(2):
            for side, by in ((0, 1), (1, -1)):
                rs[k, h, side].wait_recv()
                to = (k,) + group(h, by) + (slice(None),)
                add_into(to + (cols_of(h, side),), (s1.at[k, h, side],))
                rs_send_one(k, h, 2 + side, part.at[to + (cols_of(h, None),)],
                            s2.at[k, h, side], near(h, 2, by))

    def r3(k):
        for h in range(2):
            rs[k, h, 2].wait_recv()
            rs[k, h, 3].wait_recv()
            far = (k,) + own(h, 2) + (slice(None),)
            mine = (k,) + group(h, 0) + (slice(None), cols_of(h, None))
            add_into(mine, (s2.at[k, h, 0], s2.at[k, h, 1]))
            rs_send_one(k, h, 4, part.at[far + (cols_of(h, 0),)], t1.at[k, h, 0], near(h, 1, 1))
            rs_send_one(k, h, 5, part.at[far + (cols_of(h, 1),)], t1.at[k, h, 1], near(h, 1, -1))

    def r4(k):
        for h in range(2):
            for side, by in ((0, 1), (1, -1)):
                rs[k, h, 4 + side].wait_recv()
                to = (k,) + own(h, by) + (slice(None),)
                add_into(to + (cols_of(h, side),), (t1.at[k, h, side],))
                rs_send_one(k, h, 6 + side, part.at[to + (cols_of(h, None),)],
                            t2.at[k, h, side], near(h, 1, by))

    rt = {}

    def r5(k):
        for h in range(2):
            rs[k, h, 6].wait_recv()
            rs[k, h, 7].wait_recv()
            value = part[(k, z, x, slice(None), cols_of(h, None))].astype(F32)
            value += t2[k, h, 0].astype(F32) + t2[k, h, 1].astype(F32)
            for q in range(4):
                at = (4 * h + q) * BLOCK
                fin[at:at + BLOCK, :eighth] = value[:, q * eighth:(q + 1) * eighth].astype(BF16)
        span = pl.ds(0, eighth)
        if k == 0:
            fin[CHUNKS * BLOCK:, eighth:] = jnp.zeros((slots - CHUNKS * BLOCK, LANES), BF16)
        if k == CHUNKS - 1:
            span = pl.ds(0, eighth + LANES)
            for d in range(1, SIDE * SIDE):
                pp[d].wait_recv()
            ppr[0] = pps[z, x]
            summed = jnp.sum(ppr[...], axis=0)[:1]
            held = CHUNKS * BLOCK
            diagonal = iota((held, LANES), 0) == iota((held, LANES), 1)
            column = jnp.sum(
                jnp.where(diagonal, jnp.broadcast_to(summed, (held, LANES)), 0.0),
                axis=1, keepdims=True,
            )
            column = jnp.broadcast_to(column, (held, LANES)).astype(BF16)
            fin[:held, eighth:] = column
        row, col = iota((slots, slots), 0), iota((slots, slots), 1)
        inner = row % BLOCK
        place = (inner // PAIR) * BLOCK + (row // BLOCK) * PAIR + inner % PAIR
        moved = dot(select(col == place), fin[:, span]).astype(BF16)
        rsnd[k, :, :, span] = moved.reshape(OWNERS, BLOCK, moved.shape[1])
        for dc in range(1, OWNERS):
            to = (c + dc) % OWNERS
            rt[k, dc] = send(
                rsnd.at[k, to, :, span], rrcv.at[k, c, :, span],
                rt_send.at[k, dc], rt_recv.at[k, dc], {"ctx": to, "tp": t},
            )
        rrcv[k, c, :, span] = rsnd[k, c, :, span]

    pp = {}

    def probs_out():
        for d in range(1, SIDE * SIDE):
            xd, zd = step(x, d // SIDE), step(z, d % SIDE)
            pp[d] = send(pps.at[zd, xd], ppr.at[d], pp_send.at[d], pp_recv.at[d], at_xz(xd, zd))

    def weight_in(first, last):
        @pl.loop(first, last)
        def _(i):
            at = pl.ds(pl.multiple_of(i * wide, wide), wide)
            rows_in = ga[:, :, :, :, at].reshape(CHUNKS * ROWS, wide)
            value = dot_tn(rows_in, dd[...])
            wg[at, :] = value[:, :units].astype(BF16)
            wu[at, :] = value[:, units:].astype(BF16)

    def weight_down():
        @pl.loop(0, width // wide)
        def _(i):
            at = pl.ds(pl.multiple_of(i * wide, wide), wide)
            rows_grad = gb[:, :, :, :, at].reshape(CHUNKS * ROWS, wide)
            wd[:, at] = dot_tn(wei[...], rows_grad).astype(BF16)

    for copy in stacking:
        copy.wait()
    build(0)
    pl.semaphore_wait(barrier, OWNERS - 1 + SIDE * SIDE - 1)
    disperse(0)
    build(1)
    disperse(1)
    build(2)
    disperse(2)
    assemble(0)
    g1(0)
    assemble(1)
    g1(1)
    g2(0)
    assemble(2)
    g1(2)
    g3(0)
    g2(1)
    g3(1)
    g2(2)
    g4(0)
    g3(2)
    for copy in loads:
        copy.wait()
    g5(0)
    forward(0)
    backward(0)
    r1(0)
    g4(1)
    r2(0)
    g5(1)
    g4(2)
    forward(1)
    backward(1)
    r1(1)
    r3(0)
    r2(1)
    r4(0)
    g5(2)
    forward(2)
    backward(2)
    r1(2)
    probs_out()
    r3(1)
    r5(0)
    weight_in(0, 3)
    r2(2)
    r4(1)
    weight_in(3, 6)
    r3(2)
    r5(1)
    weight_in(6, 8)
    r4(2)
    weight_in(8, 10)
    r5(2)
    weight_down()

    row, col = iota((8 * count, slots), 0), iota((8 * count, slots), 1)
    inner = col % BLOCK
    base = (col // BLOCK) * CAPACITY + inner % PAIR
    here = inner // PAIR == row // count
    spread = jnp.where(
        iota((8 * count, count), 0) % count == iota((8 * count, count), 1),
        jnp.broadcast_to(target_row[:, :count], (8 * count, count)), 0.0,
    )
    aimed = jnp.broadcast_to(jnp.sum(spread, axis=1, keepdims=True), (8 * count, slots))
    total = jnp.zeros((8 * count, eighth), F32)
    for k in range(CHUNKS):
        hit = select(here & (aimed == (base + PAIR * k).astype(F32)))
        for dc in range(1, OWNERS):
            rt[k, dc].wait_recv()
        total += dot(hit, rrcv[k, :, :, :eighth].reshape(slots, eighth))
    for q in range(8):
        out_tokens[:, q * eighth:(q + 1) * eighth] = (
            total[q * count:(q + 1) * count].astype(BF16)
        )
    col = iota((count, slots), 1)
    inner = col % BLOCK
    wanted = (col // BLOCK) * CAPACITY + inner
    hit = (inner < CAPACITY) & (jnp.broadcast_to(target, (count, slots)) == wanted.astype(F32))
    total = dot(select(hit), rrcv[CHUNKS - 1, :, :, eighth:].reshape(slots, LANES))
    eye = iota((count, count), 0) == iota((count, count), 1)
    spread = jnp.where(eye, jnp.broadcast_to(total[:, :1], (count, count)), 0.0)
    out_prob[...] = jnp.sum(spread, axis=0, keepdims=True).astype(BF16)

    for copy in sent:
        copy.wait_send()


def place(*refs):
    sources, targets, sem = refs[:5], refs[5:10], refs[10]
    copies = [
        pltpu.make_async_copy(src, dst, sem.at[i])
        for i, (src, dst) in enumerate(zip(sources, targets))
    ]
    for copy in copies:
        copy.start()
    for copy in copies:
        copy.wait()


def per_device(tokens, grad_out, gate_prob, expert_ids, w_gate, w_up, w_down):
    count, width = tokens.shape
    units = w_gate.shape[2]
    quarter, eighth, half = width // 4, width // 8, width // 2
    vmem = pl.BlockSpec(memory_space=pltpu.VMEM)
    anywhere = pl.BlockSpec(memory_space=pl.ANY)
    rows = CHUNKS * ROWS
    dma = pltpu.SemaphoreType.DMA
    made = pl.pallas_call(
        kernel,
        out_shape=(
            pltpu.VMEM((count, width), BF16),
            pltpu.VMEM((1, count), BF16),
            pltpu.VMEM(w_gate.shape, BF16),
            pltpu.VMEM(w_up.shape, BF16),
            pltpu.VMEM(w_down.shape, BF16),
        ),
        in_specs=[anywhere] * 2 + [vmem] * 2 + [anywhere] * 3,
        out_specs=[vmem] * 5,
        scratch_shapes=[
            pltpu.VMEM((8 * count, quarter + LANES), BF16),
            pltpu.VMEM((CHUNKS, OWNERS, BLOCK, quarter + LANES), BF16),
            pltpu.VMEM((CHUNKS, OWNERS, BLOCK, quarter + LANES), BF16),
            pltpu.VMEM((CHUNKS, SIDE, SIDE, BLOCK, width + LANES), BF16),
            pltpu.VMEM((CHUNKS, SIDE, SIDE, BLOCK, width), BF16),
            pltpu.VMEM((CHUNKS, SIDE, SIDE, BLOCK, width), BF16),
            pltpu.VMEM((CHUNKS, 2, 2, SIDE, BLOCK, quarter), BF16),
            pltpu.VMEM((CHUNKS, 2, 2, SIDE, BLOCK, half), BF16),
            pltpu.VMEM((CHUNKS, 2, 2, BLOCK, quarter), BF16),
            pltpu.VMEM((CHUNKS, 2, 2, BLOCK, half), BF16),
            pltpu.VMEM((8 * BLOCK, eighth + LANES), BF16),
            pltpu.VMEM((CHUNKS, OWNERS, BLOCK, eighth + LANES), BF16),
            pltpu.VMEM((CHUNKS, OWNERS, BLOCK, eighth + LANES), BF16),
            pltpu.VMEM((3, ROWS, units), F32),
            pltpu.VMEM((rows, 2 * units), BF16),
            pltpu.VMEM((rows, units), BF16),
            pltpu.VMEM((SIDE, SIDE, 8, LANES), F32),
            pltpu.VMEM((SIDE * SIDE, 8, LANES), F32),
            dma((8,)),
            dma((3,)),
            dma((CHUNKS, OWNERS)),
            dma((CHUNKS, OWNERS)),
            dma((CHUNKS, 2, 8)),
            dma((CHUNKS, 2, 8)),
            dma((CHUNKS, 2, 8)),
            dma((CHUNKS, 2, 8)),
            dma((SIDE * SIDE,)),
            dma((SIDE * SIDE,)),
            dma((CHUNKS, OWNERS)),
            dma((CHUNKS, OWNERS)),
        ],
        compiler_params=pltpu.CompilerParams(
            collective_id=0, has_side_effects=True, vmem_limit_bytes=46 * 2**20
        ),
    )(tokens, grad_out, gate_prob[None], expert_ids.reshape(1, count), w_gate, w_up, w_down)
    grad_tokens, grad_prob, grad_wg, grad_wu, grad_wd = pl.pallas_call(
        place,
        out_shape=tuple(jax.ShapeDtypeStruct(part.shape, BF16) for part in made),
        in_specs=[anywhere] * 5,
        out_specs=[anywhere] * 5,
        scratch_shapes=[dma((5,))],
        compiler_params=pltpu.CompilerParams(vmem_limit_bytes=2**20),
    )(*made)
    return grad_tokens, grad_prob[0], grad_wg, grad_wu, grad_wd


def solution(mesh):
    in_specs = (
        P(("ctx", "tp"), None),
        P(("ctx", "tp"), None),
        P(("ctx", "tp")),
        P(("ctx", "tp"), None),
        P("ctx", None, "tp"),
        P("ctx", None, "tp"),
        P("ctx", "tp", None),
    )
    out_specs = (
        P(("ctx", "tp"), None),
        P(("ctx", "tp")),
        P("ctx", None, "tp"),
        P("ctx", None, "tp"),
        P("ctx", "tp", None),
    )
    return jax.shard_map(
        per_device, mesh=mesh, in_specs=in_specs, out_specs=out_specs, check_vma=False
    )
```

```python
import jax
import jax.numpy as jnp
from jax import lax
from jax.experimental import pallas as pl
from jax.experimental.pallas import tpu as pltpu
from jax.sharding import PartitionSpec as P

F32 = jnp.float32
BF16 = jnp.bfloat16
SIDE = 4
OWNERS = 8
PAIR = 2
CHUNKS = 3
CAPACITY = PAIR * CHUNKS
BLOCK = OWNERS * PAIR
ROWS = SIDE * SIDE * BLOCK
LANES = 128


def dot(a, b):
    return jnp.dot(a, b, preferred_element_type=F32)


def dot_nt(a, b):
    return lax.dot_general(a, b, (((1,), (1,)), ((), ())), preferred_element_type=F32)


def dot_tn(a, b):
    return lax.dot_general(a, b, (((0,), (0,)), ((), ())), preferred_element_type=F32)


def iota(shape, dim):
    return lax.broadcasted_iota(jnp.int32, shape, dim)


def select(mask):
    return jnp.where(mask, 1.0, 0.0).astype(BF16)


def column(line):
    count = line.shape[1]
    eye = iota((count, count), 0) == iota((count, count), 1)
    spread = jnp.broadcast_to(line[...].astype(F32), (count, count))
    return jnp.sum(jnp.where(eye, spread, 0.0), axis=1, keepdims=True)


def targets(ids):
    count = ids.shape[1]
    chosen = column(ids)
    onehot = jnp.where(chosen == iota((count, LANES), 1).astype(F32), 1.0, 0.0)
    lower = select(iota((count, count), 0) >= iota((count, count), 1))
    ranks = dot(lower, onehot.astype(BF16))
    slot = jnp.sum(ranks * onehot, axis=1, keepdims=True) - 1.0
    return chosen * CAPACITY + slot


def kernel(
    tokens, grads, prob, ids, wg_in, wu_in, wd_in,
    rrcv, out_wg, out_wu, out_wd,
    stk, snd, rcv, ga, gb, part, s1, s2, t1, t2, fin, rsnd,
    acc, dd, wei, pps, ppr,
    i_sem, w_sem, p1_send, p1_recv, ag_send, ag_recv, rs_send, rs_recv,
    pp_send, pp_recv, rt_send, rt_recv,
):
    count, width = tokens.shape
    wg, wu, wd = out_wg.at[0], out_wu.at[0], out_wd.at[0]
    units = wg.shape[1]
    quarter, eighth, half = width // 4, width // 8, width // 2
    c = lax.axis_index("ctx")
    t = lax.axis_index("tp")
    x, z = t // SIDE, t % SIDE

    def at_xz(xd, zd):
        return {"ctx": c, "tp": xd * SIDE + zd}

    def step(p, by):
        return (p + by + SIDE) % SIDE

    barrier = pltpu.get_barrier_semaphore()
    for dc in range(1, OWNERS):
        pl.semaphore_signal(
            barrier, inc=1, device_id={"ctx": (c + dc) % OWNERS, "tp": t},
            device_id_type=pl.DeviceIdType.MESH,
        )
    for d in range(1, SIDE * SIDE):
        pl.semaphore_signal(
            barrier, inc=1, device_id=at_xz(step(x, d // SIDE), step(z, d % SIDE)),
            device_id_type=pl.DeviceIdType.MESH,
        )

    stacking = [
        pltpu.make_async_copy(
            src.at[:, q * quarter:(q + 1) * quarter],
            stk.at[pl.ds((2 * q + n) * count, count), pl.ds(0, quarter)],
            i_sem.at[2 * q + n],
        )
        for q in range(4)
        for n, src in enumerate((tokens, grads))
    ]
    for copy in stacking:
        copy.start()
    loads = [
        pltpu.make_async_copy(src, dst, w_sem.at[i])
        for i, (src, dst) in enumerate(((wg_in.at[0], wg), (wu_in.at[0], wu), (wd_in.at[0], wd)))
    ]
    for copy in loads:
        copy.start()

    sent = []

    def drain(keep=0):
        while len(sent) > keep:
            sent.pop(0).wait_send()

    def send(src, dst, send_sem, recv_sem, device):
        copy = pltpu.make_async_remote_copy(
            src_ref=src, dst_ref=dst, send_sem=send_sem, recv_sem=recv_sem,
            device_id=device, device_id_type=pl.DeviceIdType.MESH,
        )
        copy.start()
        sent.append(copy)
        return copy

    deck = 8 * count

    target = targets(ids)
    target_row = jnp.sum(
        jnp.where(
            iota((count, deck), 0) == iota((count, deck), 1) % count,
            jnp.broadcast_to(target, (count, deck)), 0.0,
        ),
        axis=0, keepdims=True,
    )
    stk[:, quarter:] = jnp.zeros((deck, LANES), BF16)
    stk[:count, quarter:] = jnp.broadcast_to(column(prob), (count, LANES)).astype(BF16)
    slots = OWNERS * BLOCK

    def build(k):
        row, col = iota((slots, deck), 0), iota((slots, deck), 1)
        inner = row % BLOCK
        want = (row // BLOCK) * CAPACITY + PAIR * k + inner % PAIR
        hit = jnp.broadcast_to(target_row, (slots, deck)) == want.astype(F32)
        pick = select(hit & (inner // PAIR == col // count))
        snd[k] = dot(pick, stk[...]).astype(BF16).reshape(OWNERS, BLOCK, quarter + LANES)

    p1 = {}

    def disperse(k):
        for dc in range(1, OWNERS):
            to = (c + dc) % OWNERS
            p1[k, dc] = send(
                snd.at[k, to], rcv.at[k, c], p1_send.at[k, dc], p1_recv.at[k, dc],
                {"ctx": to, "tp": t},
            )
        rcv[k, c] = snd[k, c]

    def assemble(k):
        for dc in range(1, OWNERS):
            p1[k, dc].wait_recv()
        row, col = iota((slots, slots), 0), iota((slots, slots), 1)
        one = row % BLOCK
        where = (one // PAIR) * BLOCK + (row // BLOCK) * PAIR + one % PAIR
        got = dot(select(col == where), rcv[k].reshape(slots, quarter + LANES)).astype(BF16)
        for q in range(4):
            cols = slice(q * quarter, (q + 1) * quarter)
            ga[k, z, x, :, cols] = got[2 * q * BLOCK:(2 * q + 1) * BLOCK, :quarter]
            gb[k, z, x, :, cols] = got[(2 * q + 1) * BLOCK:(2 * q + 2) * BLOCK, :quarter]
        ga[k, z, x, :, width:] = got[:BLOCK, quarter:]

    ag = {}
    halves = (
        (pl.ds(0, half), pl.ds(half, half + LANES)),
        (pl.ds(0, half), pl.ds(half, half)),
    )

    def ag_send_one(k, arr, n, ref, device):
        ag[k, arr, n] = send(ref, ref, ag_send.at[k, arr, n], ag_recv.at[k, arr, n], device)

    def near(arr, stage, by):
        along_x = (arr == 0) == (stage == 1)
        return at_xz(step(x, by), z) if along_x else at_xz(x, step(z, by))

    BOTH = ((0, 1), (1, -1))
    AROUND = (0, -1, 1, 2)

    def block(k, arr, first, second, cols=None):
        xd, zd = (step(x, first), step(z, second)) if arr == 0 else (step(x, second), step(z, first))
        buf = (ga, gb)[arr]
        return buf.at[k, zd, xd] if cols is None else buf.at[k, zd, xd, :, cols]

    def across(k, arr, n):
        for side, by in ((0, 1), (1, -1)):
            ag_send_one(k, arr, 4 + 2 * n + side, block(k, arr, AROUND[n], 0), near(arr, 2, by))

    def g1(k):
        for arr in range(2):
            ag_send_one(k, arr, 0, block(k, arr, 0, 0), near(arr, 1, 1))
            ag_send_one(k, arr, 1, block(k, arr, 0, 0), near(arr, 1, -1))
        for arr in range(2):
            across(k, arr, 0)

    def g2(k, arr, side):
        by = BOTH[side][1]
        ag[k, arr, side].wait_recv()
        ag_send_one(k, arr, 2 + side, block(k, arr, -by, 0, halves[arr][side]), near(arr, 1, by))
        across(k, arr, 1 + side)

    def g3(k, arr):
        ag[k, arr, 2].wait_recv()
        ag[k, arr, 3].wait_recv()
        across(k, arr, 3)

    def g4(k, arr, n, side):
        by = BOTH[side][1]
        ag[k, arr, 4 + 2 * n + side].wait_recv()
        ag_send_one(
            k, arr, 12 + 2 * n + side,
            block(k, arr, AROUND[n], -by, halves[arr][side]), near(arr, 2, by),
        )

    def g5(k):
        for arr in range(2):
            for n in range(12, 20):
                ag[k, arr, n].wait_recv()

    deep = quarter
    wide = width // 10

    def products(k, first, last):
        def one(i, fresh):
            at = pl.ds(pl.multiple_of(i * deep, deep), deep)
            rows_in = ga[k, :, :, :, at].reshape(ROWS, deep)
            rows_grad = gb[k, :, :, :, at].reshape(ROWS, deep)
            gu = dot(rows_in, jnp.concatenate([wg[at, :], wu[at, :]], axis=1))
            raw = dot_nt(rows_grad, wd[:, at])
            acc[:, :2 * units] = gu if fresh else acc[:, :2 * units] + gu
            acc[:, 2 * units:] = raw if fresh else acc[:, 2 * units:] + raw

        if first == 0:
            one(0, True)
            first = 1

        @pl.loop(first, last)
        def _(i):
            one(i, False)

    def forward(k):
        part_rows = 2 * LANES // 4

        @pl.loop(0, ROWS // part_rows)
        def _(i):
            at = pl.ds(pl.multiple_of(i * part_rows, part_rows), part_rows)
            keep = pl.ds(pl.multiple_of(k * ROWS + i * part_rows, part_rows), part_rows)
            g, u, raw = acc[at, :units], acc[at, units:2 * units], acc[at, 2 * units:]
            sig = jax.nn.sigmoid(g)
            act = g * sig
            hidden = act * u
            probs = ga[k, i, :, :, width:].reshape(part_rows, LANES).astype(F32)[:, :1]
            wei[keep, :] = (probs * hidden).astype(BF16)
            dh = probs * raw
            dd[keep, :units] = (dh * u * sig * (1.0 + g * (1.0 - sig))).astype(BF16)
            dd[keep, units:] = (dh * act).astype(BF16)
            sums = jnp.broadcast_to(
                jnp.sum(hidden * raw, axis=1, keepdims=True), (part_rows, LANES)
            )
            spot = iota((part_rows, LANES), 1) == k * BLOCK + iota((part_rows, LANES), 0) % BLOCK
            lanes = jnp.sum(
                jnp.where(spot, sums, 0.0).reshape(SIDE, BLOCK, LANES), axis=1, keepdims=True
            )
            lanes = jnp.broadcast_to(lanes, (SIDE, 8, LANES))
            pps[i] = lanes if k == 0 else pps[i] + lanes

    def backward(k, p, h):
        rows = dd[k * ROWS:(k + 1) * ROWS, :]

        if True:
            at = pl.ds(h * half + p * quarter, quarter)
            value = dot_nt(rows, jnp.concatenate([wg[at, :], wu[at, :]], axis=1))
            part[k, :, :, :, at] = value.astype(BF16).reshape(SIDE, SIDE, BLOCK, quarter)

    rs = {}

    def rs_send_one(k, h, p, n, src, dst, device):
        m = 2 * h + p
        rs[k, m, n] = send(src, dst, rs_send.at[k, m, n], rs_recv.at[k, m, n], device)

    def cols_of(h, p, side=None):
        at = h * half + p * quarter
        return slice(at, at + quarter) if side is None else slice(at + side * eighth, at + (side + 1) * eighth)

    def group(h, by):
        return (step(z, by), slice(None)) if h == 0 else (slice(None), step(x, by))

    def own(h, by):
        return (z, step(x, by)) if h == 0 else (step(z, by), x)

    def add_into(where, others):
        value = part[where].astype(F32)
        for other in others:
            value += other[...].astype(F32)
        part[where] = value.astype(BF16)

    def r1(k, p, h):
        far = (k,) + group(h, 2) + (slice(None),)
        for side, by in BOTH:
            rs_send_one(k, h, p, side, part.at[far + (cols_of(h, p, side),)],
                        s1.at[k, 2 * h + p, side], near(h, 2, by))

    def r2(k, p, h, side):
        by = BOTH[side][1]
        rs[k, 2 * h + p, side].wait_recv()
        to = (k,) + group(h, by) + (slice(None),)
        add_into(to + (cols_of(h, p, side),), (s1.at[k, 2 * h + p, side],))
        rs_send_one(k, h, p, 2 + side, part.at[to + (cols_of(h, p),)],
                    s2.at[k, 2 * h + p, side], near(h, 2, by))

    def r3(k, p, h):
        m = 2 * h + p
        rs[k, m, 2].wait_recv()
        rs[k, m, 3].wait_recv()
        far = (k,) + own(h, 2) + (slice(None),)
        mine = (k,) + group(h, 0) + (slice(None), cols_of(h, p))
        add_into(mine, (s2.at[k, m, 0], s2.at[k, m, 1]))
        for side, by in BOTH:
            rs_send_one(k, h, p, 4 + side, part.at[far + (cols_of(h, p, side),)],
                        t1.at[k, m, side], near(h, 1, by))

    def r4(k, p, h, side):
        m = 2 * h + p
        by = BOTH[side][1]
        rs[k, m, 4 + side].wait_recv()
        to = (k,) + own(h, by) + (slice(None),)
        add_into(to + (cols_of(h, p, side),), (t1.at[k, m, side],))
        rs_send_one(k, h, p, 6 + side, part.at[to + (cols_of(h, p),)],
                    t2.at[k, m, side], near(h, 1, by))

    rt = {}

    def r5(k):
        for m in range(4):
            rs[k, m, 6].wait_recv()
            rs[k, m, 7].wait_recv()
            value = part[(k, z, x, slice(None), cols_of(m // 2, m % 2))].astype(F32)
            value += t2[k, m, 0].astype(F32) + t2[k, m, 1].astype(F32)
            for q in range(2):
                at = (2 * m + q) * BLOCK
                fin[at:at + BLOCK, :eighth] = value[:, q * eighth:(q + 1) * eighth].astype(BF16)
        span = pl.ds(0, eighth)
        if k == 0:
            fin[CHUNKS * BLOCK:, eighth:] = jnp.zeros((slots - CHUNKS * BLOCK, LANES), BF16)
        if k == CHUNKS - 1:
            span = pl.ds(0, eighth + LANES)
            for d in range(1, SIDE * SIDE):
                pp[d].wait_recv()
            ppr[0] = pps[z, x]
            summed = jnp.sum(ppr[...], axis=0)[:1]
            held = CHUNKS * BLOCK
            diagonal = iota((held, LANES), 0) == iota((held, LANES), 1)
            column = jnp.sum(
                jnp.where(diagonal, jnp.broadcast_to(summed, (held, LANES)), 0.0),
                axis=1, keepdims=True,
            )
            column = jnp.broadcast_to(column, (held, LANES)).astype(BF16)
            fin[:held, eighth:] = column
        row, col = iota((slots, slots), 0), iota((slots, slots), 1)
        inner = row % BLOCK
        place = (inner // PAIR) * BLOCK + (row // BLOCK) * PAIR + inner % PAIR
        moved = dot(select(col == place), fin[:, span]).astype(BF16)
        rsnd[k, :, :, span] = moved.reshape(OWNERS, BLOCK, moved.shape[1])
        for dc in range(1, OWNERS):
            to = (c + dc) % OWNERS
            rt[k, dc] = send(
                rsnd.at[k, to, :, span], rrcv.at[k, c, :, span],
                rt_send.at[k, dc], rt_recv.at[k, dc], {"ctx": to, "tp": t},
            )
        rrcv[k, c, :, span] = rsnd[k, c, :, span]

    pp = {}

    def probs_out():
        for d in range(1, SIDE * SIDE):
            xd, zd = step(x, d // SIDE), step(z, d % SIDE)
            pp[d] = send(pps.at[zd, xd], ppr.at[d], pp_send.at[d], pp_recv.at[d], at_xz(xd, zd))

    def weight_in(first, last):
        @pl.loop(first, last)
        def _(i):
            at = pl.ds(pl.multiple_of(i * wide, wide), wide)
            rows_in = ga[:, :, :, :, at].reshape(CHUNKS * ROWS, wide)
            value = dot_tn(rows_in, dd[...])
            wg[at, :] = value[:, :units].astype(BF16)
            wu[at, :] = value[:, units:].astype(BF16)

    def weight_down(first, last):
        @pl.loop(first, last)
        def _(i):
            at = pl.ds(pl.multiple_of(i * wide, wide), wide)
            rows_grad = gb[:, :, :, :, at].reshape(CHUNKS * ROWS, wide)
            wd[:, at] = dot_tn(wei[...], rows_grad).astype(BF16)

    for copy in stacking:
        copy.wait()
    build(0)
    pl.semaphore_wait(barrier, OWNERS - 1 + SIDE * SIDE - 1)
    disperse(0)
    build(1)
    build(2)
    assemble(0)
    g1(0)
    disperse(1)
    g2(0,0,0)
    g2(0,0,1)
    g2(0,1,0)
    g2(0,1,1)
    g4(0,1,0,0)
    g4(0,1,0,1)
    g4(0,0,0,0)
    g4(0,0,0,1)
    g3(0,0)
    g4(0,0,1,0)
    g4(0,0,1,1)
    g4(0,1,1,0)
    g4(0,1,1,1)
    assemble(1)
    g1(1)
    disperse(2)
    g4(0,0,2,0)
    g4(0,0,2,1)
    g4(0,1,2,0)
    g4(0,1,2,1)
    g3(0,1)
    g4(0,0,3,0)
    g4(0,0,3,1)
    g2(1,0,0)
    g2(1,0,1)
    g4(1,1,0,0)
    g4(1,1,0,1)
    g2(1,1,0)
    g2(1,1,1)
    g4(1,0,0,0)
    g4(1,0,0,1)
    g4(0,1,3,0)
    g4(0,1,3,1)
    g3(1,0)
    g4(1,0,1,0)
    g4(1,0,1,1)
    g4(1,1,1,0)
    g4(1,1,1,1)
    assemble(2)
    g1(2)
    g4(1,0,2,0)
    g4(1,0,2,1)
    g4(1,1,2,0)
    g4(1,1,2,1)
    g3(1,1)
    g5(0)
    for copy in loads:
        copy.wait()
    products(0,0,3)
    g4(1,0,3,0)
    products(0,3,4)
    g4(1,0,3,1)
    g2(2,0,0)
    g2(2,0,1)
    forward(0)
    backward(0,0,0)
    backward(0,0,1)
    backward(0,1,0)
    g4(2,1,0,0)
    backward(0,1,1)
    g2(2,1,0)
    g4(2,1,0,1)
    g2(2,1,1)
    g4(2,0,0,0)
    g4(2,0,0,1)
    g4(1,1,3,0)
    g4(1,1,3,1)
    g3(2,0)
    g4(2,1,1,1)
    g4(2,0,1,0)
    g4(2,0,1,1)
    g4(2,1,1,0)
    g4(2,0,2,0)
    g4(2,0,2,1)
    g4(2,1,2,0)
    g4(2,1,2,1)
    g3(2,1)
    g5(1)
    r1(0,0,0)
    r1(0,0,1)
    r1(0,1,0)
    r1(0,1,1)
    products(1,0,3)
    g4(2,0,3,0)
    products(1,3,4)
    g4(2,0,3,1)
    forward(1)
    g4(2,1,3,0)
    backward(1,0,0)
    g4(2,1,3,1)
    backward(1,0,1)
    backward(1,1,0)
    r2(0,0,1,0)
    r2(0,0,1,1)
    r2(0,0,0,0)
    backward(1,1,1)
    r2(0,1,1,0)
    r2(0,0,0,1)
    r2(0,1,1,1)
    r2(0,1,0,0)
    r2(0,1,0,1)
    g5(2)
    r1(1,0,0)
    r1(1,0,1)
    r1(1,1,0)
    r1(1,1,1)
    products(2,0,1)
    r3(0,0,1)
    products(2,1,2)
    r3(0,0,0)
    products(2,2,3)
    r3(0,1,1)
    products(2,3,4)
    r3(0,1,0)
    r2(1,0,0,0)
    r2(1,0,1,0)
    r2(1,0,1,1)
    forward(2)
    r4(0,0,0,0)
    r4(0,0,0,1)
    r2(1,0,0,1)
    r2(1,1,0,0)
    r2(1,1,1,0)
    r4(0,0,1,0)
    r2(1,1,1,1)
    r4(0,1,0,0)
    r4(0,1,0,1)
    r4(0,1,1,0)
    r2(1,1,0,1)
    r4(0,0,1,1)
    backward(2,0,0)
    r4(0,1,1,1)
    r1(2,0,0)
    backward(2,0,1)
    r1(2,0,1)
    backward(2,1,0)
    r1(2,1,0)
    backward(2,1,1)
    r3(1,0,1)
    r1(2,1,1)
    probs_out()
    r3(1,0,0)
    weight_in(0,3)
    r3(1,1,0)
    r3(1,1,1)
    weight_in(3,4)
    r2(2,0,0,0)
    r2(2,0,1,0)
    r2(2,0,1,1)
    r5(0)
    r4(1,0,0,0)
    r4(1,0,0,1)
    r4(1,0,1,0)
    r4(1,1,0,0)
    r4(1,1,0,1)
    r4(1,1,1,0)
    r2(2,0,0,1)
    r2(2,1,0,0)
    r2(2,1,0,1)
    r4(1,0,1,1)
    r2(2,1,1,0)
    r2(2,1,1,1)
    r4(1,1,1,1)
    weight_in(4,7)
    r3(2,0,1)
    weight_in(7,9)
    r3(2,0,0)
    weight_in(9,10)
    weight_down(0,2)
    r4(2,0,1,0)
    r3(2,1,1)
    r3(2,1,0)
    r4(2,0,0,0)
    r4(2,0,0,1)
    weight_down(2,4)
    r5(1)
    r4(2,0,1,1)
    r4(2,1,0,0)
    r4(2,1,0,1)
    r4(2,1,1,0)
    r4(2,1,1,1)
    weight_down(4,10)
    r5(2)

    for k in range(CHUNKS):
        for dc in range(1, OWNERS):
            rt[k, dc].wait_recv()
    drain()


def finish(
    ids, back_in, wg, wu, wd, tokens_out, out_prob, out_wg, out_wu, out_wd,
    back, out_tokens, sem,
):
    copies = [
        pltpu.make_async_copy(src, dst, sem.at[i])
        for i, (src, dst) in enumerate(
            ((back_in, back), (wg, out_wg), (wu, out_wu), (wd, out_wd))
        )
    ]
    for copy in copies:
        copy.start()
    count = ids.shape[1]
    eighth = back.shape[3] - LANES
    slots = OWNERS * BLOCK
    target = targets(ids)
    aimed = jnp.broadcast_to(jnp.concatenate([target] * 8, axis=0), (8 * count, slots))
    row, col = iota((8 * count, slots), 0), iota((8 * count, slots), 1)
    inner = col % BLOCK
    base = (col // BLOCK) * CAPACITY + inner % PAIR
    here = inner // PAIR == row // count
    copies.pop(0).wait()
    total = jnp.zeros((8 * count, eighth), F32)
    for k in range(CHUNKS):
        hit = select(here & (aimed == (base + PAIR * k).astype(F32)))
        total += dot(hit, back[k, :, :, :eighth].reshape(slots, eighth))
    for q in range(8):
        out_tokens[:, q * eighth:(q + 1) * eighth] = (
            total[q * count:(q + 1) * count].astype(BF16)
        )
    copies.append(pltpu.make_async_copy(out_tokens, tokens_out, sem.at[4]))
    copies[-1].start()
    col = iota((count, slots), 1)
    inner = col % BLOCK
    wanted = (col // BLOCK) * CAPACITY + inner
    hit = (inner < CAPACITY) & (jnp.broadcast_to(target, (count, slots)) == wanted.astype(F32))
    total = dot(select(hit), back[CHUNKS - 1, :, :, eighth:].reshape(slots, LANES))
    eye = iota((count, count), 0) == iota((count, count), 1)
    spread = jnp.where(eye, jnp.broadcast_to(total[:, :1], (count, count)), 0.0)
    out_prob[...] = jnp.sum(spread, axis=0, keepdims=True).astype(BF16)
    for copy in copies:
        copy.wait()


def per_device(tokens, grad_out, gate_prob, expert_ids, w_gate, w_up, w_down):
    count, width = tokens.shape
    units = w_gate.shape[2]
    quarter, eighth, half = width // 4, width // 8, width // 2
    vmem = pl.BlockSpec(memory_space=pltpu.VMEM)
    anywhere = pl.BlockSpec(memory_space=pl.ANY)
    rows = CHUNKS * ROWS
    dma = pltpu.SemaphoreType.DMA
    ids = expert_ids.reshape(1, count)
    back, *made = pl.pallas_call(
        kernel,
        out_shape=(
            pltpu.VMEM((CHUNKS, OWNERS, BLOCK, eighth + LANES), BF16),
            pltpu.VMEM(w_gate.shape, BF16),
            pltpu.VMEM(w_up.shape, BF16),
            pltpu.VMEM(w_down.shape, BF16),
        ),
        in_specs=[anywhere] * 2 + [vmem] * 2 + [anywhere] * 3,
        out_specs=[vmem] * 4,
        scratch_shapes=[
            pltpu.VMEM((8 * count, quarter + LANES), BF16),
            pltpu.VMEM((CHUNKS, OWNERS, BLOCK, quarter + LANES), BF16),
            pltpu.VMEM((CHUNKS, OWNERS, BLOCK, quarter + LANES), BF16),
            pltpu.VMEM((CHUNKS, SIDE, SIDE, BLOCK, width + LANES), BF16),
            pltpu.VMEM((CHUNKS, SIDE, SIDE, BLOCK, width), BF16),
            pltpu.VMEM((CHUNKS, SIDE, SIDE, BLOCK, width), BF16),
            pltpu.VMEM((CHUNKS, 4, 2, SIDE, BLOCK, eighth), BF16),
            pltpu.VMEM((CHUNKS, 4, 2, SIDE, BLOCK, quarter), BF16),
            pltpu.VMEM((CHUNKS, 4, 2, BLOCK, eighth), BF16),
            pltpu.VMEM((CHUNKS, 4, 2, BLOCK, quarter), BF16),
            pltpu.VMEM((8 * BLOCK, eighth + LANES), BF16),
            pltpu.VMEM((CHUNKS, OWNERS, BLOCK, eighth + LANES), BF16),
            pltpu.VMEM((ROWS, 3 * units), F32),
            pltpu.VMEM((rows, 2 * units), BF16),
            pltpu.VMEM((rows, units), BF16),
            pltpu.VMEM((SIDE, SIDE, 8, LANES), F32),
            pltpu.VMEM((SIDE * SIDE, 8, LANES), F32),
            dma((8,)),
            dma((3,)),
            dma((CHUNKS, OWNERS)),
            dma((CHUNKS, OWNERS)),
            dma((CHUNKS, 2, 20)),
            dma((CHUNKS, 2, 20)),
            dma((CHUNKS, 4, 8)),
            dma((CHUNKS, 4, 8)),
            dma((SIDE * SIDE,)),
            dma((SIDE * SIDE,)),
            dma((CHUNKS, OWNERS)),
            dma((CHUNKS, OWNERS)),
        ],
        compiler_params=pltpu.CompilerParams(
            collective_id=0, has_side_effects=True, vmem_limit_bytes=46 * 2**20
        ),
    )(tokens, grad_out, gate_prob[None], ids, w_gate, w_up, w_down)
    grad_tokens, grad_prob, *grads = pl.pallas_call(
        finish,
        out_shape=(
            jax.ShapeDtypeStruct((count, width), BF16),
            jax.ShapeDtypeStruct((1, count), BF16),
            *(jax.ShapeDtypeStruct(grad.shape, BF16) for grad in made),
        ),
        in_specs=[vmem] + [anywhere] * 4,
        out_specs=[anywhere, vmem] + [anywhere] * 3,
        scratch_shapes=[
            pltpu.VMEM(back.shape, BF16), pltpu.VMEM((count, width), BF16), dma((5,))
        ],
        compiler_params=pltpu.CompilerParams(vmem_limit_bytes=6 * 2**20),
    )(ids, back, *made)
    return (grad_tokens, grad_prob[0], *grads)


def solution(mesh):
    in_specs = (
        P(("ctx", "tp"), None),
        P(("ctx", "tp"), None),
        P(("ctx", "tp")),
        P(("ctx", "tp"), None),
        P("ctx", None, "tp"),
        P("ctx", None, "tp"),
        P("ctx", "tp", None),
    )
    out_specs = (
        P(("ctx", "tp"), None),
        P(("ctx", "tp")),
        P("ctx", None, "tp"),
        P("ctx", None, "tp"),
        P("ctx", "tp", None),
    )
    return jax.shard_map(
        per_device, mesh=mesh, in_specs=in_specs, out_specs=out_specs, check_vma=False
    )
```

```python
import jax
import jax.numpy as jnp
from jax import lax
from jax.experimental import pallas as pl
from jax.experimental.pallas import tpu as pltpu
from jax.sharding import PartitionSpec as P

F32 = jnp.float32
BF16 = jnp.bfloat16
SIDE = 4
OWNERS = 8
PAIR = 2
CHUNKS = 3
CAPACITY = PAIR * CHUNKS
BLOCK = OWNERS * PAIR
ROWS = SIDE * SIDE * BLOCK
LANES = 128


def dot(a, b):
    return jnp.dot(a, b, preferred_element_type=F32)


def dot_nt(a, b):
    return lax.dot_general(a, b, (((1,), (1,)), ((), ())), preferred_element_type=F32)


def dot_tn(a, b):
    return lax.dot_general(a, b, (((0,), (0,)), ((), ())), preferred_element_type=F32)


def iota(shape, dim):
    return lax.broadcasted_iota(jnp.int32, shape, dim)


def select(mask):
    return jnp.where(mask, 1.0, 0.0).astype(BF16)


def column(line):
    count = line.shape[1]
    eye = iota((count, count), 0) == iota((count, count), 1)
    spread = jnp.broadcast_to(line[...].astype(F32), (count, count))
    return jnp.sum(jnp.where(eye, spread, 0.0), axis=1, keepdims=True)


def targets(ids):
    count = ids.shape[1]
    chosen = column(ids)
    onehot = jnp.where(chosen == iota((count, LANES), 1).astype(F32), 1.0, 0.0)
    lower = select(iota((count, count), 0) >= iota((count, count), 1))
    ranks = dot(lower, onehot.astype(BF16))
    slot = jnp.sum(ranks * onehot, axis=1, keepdims=True) - 1.0
    return chosen * CAPACITY + slot


def kernel(
    tokens, grads, prob, ids, wg_in, wu_in, wd_in,
    rrcv, out_wg, out_wu, out_wd,
    stk, snd, rcv, ga, gb, part, s1, s2, t1, t2, t3, fin, rsnd,
    acc, dd, wei, pps, ppr,
    i_sem, w_sem, p1_send, p1_recv, ag_send, ag_recv, rs_send, rs_recv,
    pp_send, pp_recv, rt_send, rt_recv,
):
    count, width = tokens.shape
    wg, wu, wd = out_wg.at[0], out_wu.at[0], out_wd.at[0]
    units = wg.shape[1]
    quarter, eighth, half = width // 4, width // 8, width // 2
    c = lax.axis_index("ctx")
    t = lax.axis_index("tp")
    x, z = t // SIDE, t % SIDE

    def at_xz(xd, zd):
        return {"ctx": c, "tp": xd * SIDE + zd}

    def step(p, by):
        return (p + by + SIDE) % SIDE

    barrier = pltpu.get_barrier_semaphore()
    for dc in range(1, OWNERS):
        pl.semaphore_signal(
            barrier, inc=1, device_id={"ctx": (c + dc) % OWNERS, "tp": t},
            device_id_type=pl.DeviceIdType.MESH,
        )
    for d in range(1, SIDE * SIDE):
        pl.semaphore_signal(
            barrier, inc=1, device_id=at_xz(step(x, d // SIDE), step(z, d % SIDE)),
            device_id_type=pl.DeviceIdType.MESH,
        )

    stacking = [
        pltpu.make_async_copy(
            src.at[:, q * quarter:(q + 1) * quarter],
            stk.at[pl.ds((2 * q + n) * count, count), pl.ds(0, quarter)],
            i_sem.at[2 * q + n],
        )
        for q in range(4)
        for n, src in enumerate((tokens, grads))
    ]
    for copy in stacking:
        copy.start()
    loads = [
        pltpu.make_async_copy(src, dst, w_sem.at[i])
        for i, (src, dst) in enumerate(((wg_in.at[0], wg), (wu_in.at[0], wu), (wd_in.at[0], wd)))
    ]
    for copy in loads:
        copy.start()

    sent = []

    def drain(keep=0):
        while len(sent) > keep:
            sent.pop(0).wait_send()

    def send(src, dst, send_sem, recv_sem, device):
        copy = pltpu.make_async_remote_copy(
            src_ref=src, dst_ref=dst, send_sem=send_sem, recv_sem=recv_sem,
            device_id=device, device_id_type=pl.DeviceIdType.MESH,
        )
        copy.start()
        sent.append(copy)
        return copy

    deck = 8 * count

    target = targets(ids)
    target_row = jnp.sum(
        jnp.where(
            iota((count, deck), 0) == iota((count, deck), 1) % count,
            jnp.broadcast_to(target, (count, deck)), 0.0,
        ),
        axis=0, keepdims=True,
    )
    stk[:, quarter:] = jnp.zeros((deck, LANES), BF16)
    stk[:count, quarter:] = jnp.broadcast_to(column(prob), (count, LANES)).astype(BF16)
    slots = OWNERS * BLOCK

    def build(k):
        row, col = iota((slots, deck), 0), iota((slots, deck), 1)
        inner = row % BLOCK
        want = (row // BLOCK) * CAPACITY + PAIR * k + inner % PAIR
        hit = jnp.broadcast_to(target_row, (slots, deck)) == want.astype(F32)
        pick = select(hit & (inner // PAIR == col // count))
        snd[k] = dot(pick, stk[...]).astype(BF16).reshape(OWNERS, BLOCK, quarter + LANES)

    p1 = {}

    def disperse(k):
        for dc in range(1, OWNERS):
            to = (c + dc) % OWNERS
            p1[k, dc] = send(
                snd.at[k, to], rcv.at[k, c], p1_send.at[k, dc], p1_recv.at[k, dc],
                {"ctx": to, "tp": t},
            )
        rcv[k, c] = snd[k, c]

    def assemble(k):
        for dc in range(1, OWNERS):
            p1[k, dc].wait_recv()
        row, col = iota((slots, slots), 0), iota((slots, slots), 1)
        one = row % BLOCK
        where = (one // PAIR) * BLOCK + (row // BLOCK) * PAIR + one % PAIR
        got = dot(select(col == where), rcv[k].reshape(slots, quarter + LANES)).astype(BF16)
        for q in range(4):
            cols = slice(q * quarter, (q + 1) * quarter)
            ga[k, z, x, :, cols] = got[2 * q * BLOCK:(2 * q + 1) * BLOCK, :quarter]
            gb[k, z, x, :, cols] = got[(2 * q + 1) * BLOCK:(2 * q + 2) * BLOCK, :quarter]
        ga[k, z, x, :, width:] = got[:BLOCK, quarter:]

    ag = {}
    halves = (
        (pl.ds(0, half), pl.ds(half, half + LANES)),
        (pl.ds(0, half), pl.ds(half, half)),
    )

    def ag_send_one(k, arr, n, ref, device):
        ag[k, arr, n] = send(ref, ref, ag_send.at[k, arr, n], ag_recv.at[k, arr, n], device)

    def near(arr, stage, by):
        along_x = (arr == 0) == (stage == 1)
        return at_xz(step(x, by), z) if along_x else at_xz(x, step(z, by))

    BOTH = ((0, 1), (1, -1))
    AROUND = (0, -1, 1, 2)

    def block(k, arr, first, second, cols=None):
        xd, zd = (step(x, first), step(z, second)) if arr == 0 else (step(x, second), step(z, first))
        buf = (ga, gb)[arr]
        return buf.at[k, zd, xd] if cols is None else buf.at[k, zd, xd, :, cols]

    def across(k, arr, n):
        for side, by in ((0, 1), (1, -1)):
            ag_send_one(k, arr, 4 + 2 * n + side, block(k, arr, AROUND[n], 0), near(arr, 2, by))

    def g1(k):
        for arr in range(2):
            ag_send_one(k, arr, 0, block(k, arr, 0, 0), near(arr, 1, 1))
            ag_send_one(k, arr, 1, block(k, arr, 0, 0), near(arr, 1, -1))
        for arr in range(2):
            across(k, arr, 0)

    def g2(k, arr, side):
        by = BOTH[side][1]
        ag[k, arr, side].wait_recv()
        ag_send_one(k, arr, 2 + side, block(k, arr, -by, 0, halves[arr][side]), near(arr, 1, by))
        across(k, arr, 1 + side)

    def g3(k, arr):
        ag[k, arr, 2].wait_recv()
        ag[k, arr, 3].wait_recv()
        across(k, arr, 3)

    def g4(k, arr, n, side):
        by = BOTH[side][1]
        ag[k, arr, 4 + 2 * n + side].wait_recv()
        ag_send_one(
            k, arr, 12 + 2 * n + side,
            block(k, arr, AROUND[n], -by, halves[arr][side]), near(arr, 2, by),
        )

    def g5(k):
        for arr in range(2):
            for n in range(12, 20):
                ag[k, arr, n].wait_recv()

    deep = quarter
    wide = width // 10

    def products(k, first, last):
        def one(i, fresh):
            at = pl.ds(pl.multiple_of(i * deep, deep), deep)
            rows_in = ga[k, :, :, :, at].reshape(ROWS, deep)
            rows_grad = gb[k, :, :, :, at].reshape(ROWS, deep)
            gu = dot(rows_in, jnp.concatenate([wg[at, :], wu[at, :]], axis=1))
            raw = dot_nt(rows_grad, wd[:, at])
            acc[:, :2 * units] = gu if fresh else acc[:, :2 * units] + gu
            acc[:, 2 * units:] = raw if fresh else acc[:, 2 * units:] + raw

        if first == 0:
            one(0, True)
            first = 1

        @pl.loop(first, last)
        def _(i):
            one(i, False)

    def forward(k):
        part_rows = 2 * LANES // 4

        @pl.loop(0, ROWS // part_rows)
        def _(i):
            at = pl.ds(pl.multiple_of(i * part_rows, part_rows), part_rows)
            keep = pl.ds(pl.multiple_of(k * ROWS + i * part_rows, part_rows), part_rows)
            g, u, raw = acc[at, :units], acc[at, units:2 * units], acc[at, 2 * units:]
            sig = jax.nn.sigmoid(g)
            act = g * sig
            hidden = act * u
            probs = ga[k, i, :, :, width:].reshape(part_rows, LANES).astype(F32)[:, :1]
            wei[keep, :] = (probs * hidden).astype(BF16)
            dh = probs * raw
            dd[keep, :units] = (dh * u * sig * (1.0 + g * (1.0 - sig))).astype(BF16)
            dd[keep, units:] = (dh * act).astype(BF16)
            sums = jnp.broadcast_to(
                jnp.sum(hidden * raw, axis=1, keepdims=True), (part_rows, LANES)
            )
            spot = iota((part_rows, LANES), 1) == k * BLOCK + iota((part_rows, LANES), 0) % BLOCK
            lanes = jnp.sum(
                jnp.where(spot, sums, 0.0).reshape(SIDE, BLOCK, LANES), axis=1, keepdims=True
            )
            lanes = jnp.broadcast_to(lanes, (SIDE, 8, LANES))
            pps[i] = lanes if k == 0 else pps[i] + lanes

    def backward(k, p, h):
        rows = dd[k * ROWS:(k + 1) * ROWS, :]

        if True:
            at = pl.ds(h * half + p * quarter, quarter)
            value = dot_nt(rows, jnp.concatenate([wg[at, :], wu[at, :]], axis=1))
            part[k, :, :, :, at] = value.astype(BF16).reshape(SIDE, SIDE, BLOCK, quarter)

    rs = {}

    def rs_send_one(k, h, p, n, src, dst, device):
        m = 2 * h + p
        rs[k, m, n] = send(src, dst, rs_send.at[k, m, n], rs_recv.at[k, m, n], device)

    def cols_of(h, p, side=None):
        at = h * half + p * quarter
        return slice(at, at + quarter) if side is None else slice(at + side * eighth, at + (side + 1) * eighth)

    def group(h, by):
        return (step(z, by), slice(None)) if h == 0 else (slice(None), step(x, by))

    def own(h, by):
        return (z, step(x, by)) if h == 0 else (step(z, by), x)

    def add_into(where, others):
        value = part[where].astype(F32)
        for other in others:
            value += other[...].astype(F32)
        part[where] = value.astype(BF16)

    def r1(k, p, h):
        far = (k,) + group(h, 2) + (slice(None),)
        for side, by in BOTH:
            rs_send_one(k, h, p, side, part.at[far + (cols_of(h, p, side),)],
                        s1.at[k, 2 * h + p, side], near(h, 2, by))

    def r2(k, p, h, side):
        by = BOTH[side][1]
        rs[k, 2 * h + p, side].wait_recv()
        to = (k,) + group(h, by) + (slice(None),)
        add_into(to + (cols_of(h, p, side),), (s1.at[k, 2 * h + p, side],))
        rs_send_one(k, h, p, 2 + side, part.at[to + (cols_of(h, p),)],
                    s2.at[k, 2 * h + p, side], near(h, 2, by))

    def r3(k, p, h):
        m = 2 * h + p
        rs[k, m, 2].wait_recv()
        rs[k, m, 3].wait_recv()
        far = (k,) + own(h, 2) + (slice(None),)
        mine = (k,) + group(h, 0) + (slice(None), cols_of(h, p))
        add_into(mine, (s2.at[k, m, 0], s2.at[k, m, 1]))
        if k == CHUNKS - 1:
            for n, by, dst in ((6, 1, t2.at[k, m, 0]), (7, -1, t2.at[k, m, 1]), (4, 2, t3.at[m])):
                to = (k,) + own(h, by) + (slice(None), cols_of(h, p))
                rs_send_one(k, h, p, n, part.at[to], dst, near(h, 1, by))
            return
        for side, by in BOTH:
            rs_send_one(k, h, p, 4 + side, part.at[far + (cols_of(h, p, side),)],
                        t1.at[k, m, side], near(h, 1, by))

    def r4(k, p, h, side):
        m = 2 * h + p
        by = BOTH[side][1]
        rs[k, m, 4 + side].wait_recv()
        to = (k,) + own(h, by) + (slice(None),)
        add_into(to + (cols_of(h, p, side),), (t1.at[k, m, side],))
        rs_send_one(k, h, p, 6 + side, part.at[to + (cols_of(h, p),)],
                    t2.at[k, m, side], near(h, 1, by))

    rt = {}

    def r5(k):
        for m in range(4):
            rs[k, m, 6].wait_recv()
            rs[k, m, 7].wait_recv()
            value = part[(k, z, x, slice(None), cols_of(m // 2, m % 2))].astype(F32)
            value += t2[k, m, 0].astype(F32) + t2[k, m, 1].astype(F32)
            if k == CHUNKS - 1:
                rs[k, m, 4].wait_recv()
                value += t3[m].astype(F32)
            for q in range(2):
                at = (2 * m + q) * BLOCK
                fin[at:at + BLOCK, :eighth] = value[:, q * eighth:(q + 1) * eighth].astype(BF16)
        span = pl.ds(0, eighth)
        if k == 0:
            fin[CHUNKS * BLOCK:, eighth:] = jnp.zeros((slots - CHUNKS * BLOCK, LANES), BF16)
        if k == CHUNKS - 1:
            span = pl.ds(0, eighth + LANES)
            for d in range(1, SIDE * SIDE):
                pp[d].wait_recv()
            ppr[0] = pps[z, x]
            summed = jnp.sum(ppr[...], axis=0)[:1]
            held = CHUNKS * BLOCK
            diagonal = iota((held, LANES), 0) == iota((held, LANES), 1)
            column = jnp.sum(
                jnp.where(diagonal, jnp.broadcast_to(summed, (held, LANES)), 0.0),
                axis=1, keepdims=True,
            )
            column = jnp.broadcast_to(column, (held, LANES)).astype(BF16)
            fin[:held, eighth:] = column
        row, col = iota((slots, slots), 0), iota((slots, slots), 1)
        inner = row % BLOCK
        place = (inner // PAIR) * BLOCK + (row // BLOCK) * PAIR + inner % PAIR
        moved = dot(select(col == place), fin[:, span]).astype(BF16)
        rsnd[k, :, :, span] = moved.reshape(OWNERS, BLOCK, moved.shape[1])
        for dc in range(1, OWNERS):
            to = (c + dc) % OWNERS
            rt[k, dc] = send(
                rsnd.at[k, to, :, span], rrcv.at[k, c, :, span],
                rt_send.at[k, dc], rt_recv.at[k, dc], {"ctx": to, "tp": t},
            )
        rrcv[k, c, :, span] = rsnd[k, c, :, span]

    pp = {}

    def probs_out():
        for d in range(1, SIDE * SIDE):
            xd, zd = step(x, d // SIDE), step(z, d % SIDE)
            pp[d] = send(pps.at[zd, xd], ppr.at[d], pp_send.at[d], pp_recv.at[d], at_xz(xd, zd))

    def weight_in(first, last):
        @pl.loop(first, last)
        def _(i):
            at = pl.ds(pl.multiple_of(i * wide, wide), wide)
            rows_in = ga[:, :, :, :, at].reshape(CHUNKS * ROWS, wide)
            value = dot_tn(rows_in, dd[...])
            wg[at, :] = value[:, :units].astype(BF16)
            wu[at, :] = value[:, units:].astype(BF16)

    def weight_down(first, last):
        @pl.loop(first, last)
        def _(i):
            at = pl.ds(pl.multiple_of(i * wide, wide), wide)
            rows_grad = gb[:, :, :, :, at].reshape(CHUNKS * ROWS, wide)
            wd[:, at] = dot_tn(wei[...], rows_grad).astype(BF16)

    for copy in stacking:
        copy.wait()
    build(0)
    pl.semaphore_wait(barrier, OWNERS - 1 + SIDE * SIDE - 1)
    disperse(0)
    build(1)
    build(2)
    assemble(0)
    g1(0)
    disperse(1)
    g2(0,0,0)
    g2(0,0,1)
    g2(0,1,0)
    g2(0,1,1)
    assemble(1)
    g1(1)
    disperse(2)
    g4(0,1,0,0)
    g4(0,1,0,1)
    g4(0,0,0,0)
    g4(0,0,0,1)
    g3(0,0)
    g4(0,0,1,0)
    g4(0,0,1,1)
    g4(0,1,1,0)
    g4(0,1,1,1)
    g4(0,0,2,0)
    g4(0,0,2,1)
    g4(0,1,2,0)
    g4(0,1,2,1)
    g3(0,1)
    g2(1,0,0)
    g2(1,0,1)
    g2(1,1,0)
    g2(1,1,1)
    assemble(2)
    g1(2)
    g4(1,1,0,0)
    g4(1,1,0,1)
    g4(1,0,0,0)
    g4(1,0,0,1)
    g4(0,0,3,0)
    g4(0,0,3,1)
    g4(0,1,3,0)
    g4(0,1,3,1)
    g3(1,0)
    g4(1,0,1,0)
    g4(1,0,1,1)
    g4(1,1,1,0)
    g4(1,1,1,1)
    g4(1,0,2,0)
    g4(1,0,2,1)
    g4(1,1,2,0)
    g4(1,1,2,1)
    g3(1,1)
    g2(2,0,0)
    g2(2,0,1)
    g2(2,1,0)
    g2(2,1,1)
    g4(2,1,0,0)
    g4(2,1,0,1)
    g4(2,0,0,0)
    g4(2,0,0,1)
    g5(0)
    for copy in loads:
        copy.wait()
    products(0,0,3)
    g4(1,0,3,0)
    g4(1,0,3,1)
    products(0,3,4)
    forward(0)
    g4(1,1,3,0)
    g4(1,1,3,1)
    backward(0,0,0)
    backward(0,0,1)
    backward(0,1,0)
    g3(2,0)
    backward(0,1,1)
    g4(2,0,1,0)
    g4(2,0,1,1)
    g4(2,1,1,0)
    g4(2,1,1,1)
    g4(2,0,2,0)
    g4(2,0,2,1)
    g4(2,1,2,0)
    g4(2,1,2,1)
    g3(2,1)
    g5(1)
    r1(0,0,0)
    r1(0,0,1)
    r1(0,1,0)
    r1(0,1,1)
    products(1,0,2)
    g4(2,0,3,0)
    g4(2,0,3,1)
    products(1,2,4)
    g4(2,1,3,0)
    g4(2,1,3,1)
    forward(1)
    backward(1,0,0)
    r2(0,0,1,0)
    r2(0,0,1,1)
    r2(0,0,0,0)
    backward(1,0,1)
    r2(0,1,1,0)
    r2(0,0,0,1)
    r2(0,1,1,1)
    backward(1,1,0)
    r2(0,1,0,0)
    backward(1,1,1)
    r2(0,1,0,1)
    g5(2)
    r1(1,0,0)
    r1(1,0,1)
    r1(1,1,0)
    r1(1,1,1)
    products(2,0,1)
    r3(0,0,1)
    products(2,1,2)
    r3(0,0,0)
    products(2,2,3)
    r3(0,1,1)
    products(2,3,4)
    r3(0,1,0)
    r2(1,0,0,0)
    r2(1,0,1,0)
    r2(1,0,1,1)
    forward(2)
    r4(0,0,0,0)
    r4(0,0,0,1)
    r2(1,0,0,1)
    r2(1,1,0,0)
    r2(1,1,1,0)
    r4(0,0,1,0)
    r2(1,1,1,1)
    r4(0,1,0,0)
    r4(0,1,0,1)
    r4(0,1,1,0)
    r2(1,1,0,1)
    r4(0,0,1,1)
    backward(2,0,0)
    r4(0,1,1,1)
    r1(2,0,0)
    backward(2,0,1)
    r1(2,0,1)
    backward(2,1,0)
    r1(2,1,0)
    backward(2,1,1)
    r3(1,0,1)
    r1(2,1,1)
    probs_out()
    r3(1,0,0)
    weight_in(0,3)
    r3(1,1,0)
    r3(1,1,1)
    weight_in(3,4)
    r2(2,0,0,0)
    r2(2,0,1,0)
    r2(2,0,1,1)
    r5(0)
    r4(1,0,0,0)
    r4(1,0,0,1)
    r4(1,0,1,0)
    r4(1,1,0,0)
    r4(1,1,0,1)
    r4(1,1,1,0)
    r2(2,0,0,1)
    r2(2,1,0,0)
    r2(2,1,0,1)
    r4(1,0,1,1)
    r2(2,1,1,0)
    r2(2,1,1,1)
    r4(1,1,1,1)
    weight_in(4,7)
    r3(2,0,1)
    weight_in(7,9)
    r3(2,0,0)
    weight_in(9,10)
    weight_down(0,1)
    r3(2,1,1)
    weight_down(1,2)
    r3(2,1,0)
    weight_down(2,4)
    r5(1)
    weight_down(4,8)
    r5(2)
    weight_down(8,10)

    for k in range(CHUNKS):
        for dc in range(1, OWNERS):
            rt[k, dc].wait_recv()
    drain()


def finish(
    ids, back_in, wg, wu, wd, tokens_out, out_prob, out_wg, out_wu, out_wd,
    back, out_tokens, sem,
):
    copies = [
        pltpu.make_async_copy(src, dst, sem.at[i])
        for i, (src, dst) in enumerate(
            ((back_in, back), (wg, out_wg), (wu, out_wu), (wd, out_wd))
        )
    ]
    for copy in copies:
        copy.start()
    count = ids.shape[1]
    eighth = back.shape[3] - LANES
    slots = OWNERS * BLOCK
    target = targets(ids)
    aimed = jnp.broadcast_to(jnp.concatenate([target] * 8, axis=0), (8 * count, slots))
    row, col = iota((8 * count, slots), 0), iota((8 * count, slots), 1)
    inner = col % BLOCK
    base = (col // BLOCK) * CAPACITY + inner % PAIR
    here = inner // PAIR == row // count
    copies.pop(0).wait()
    total = jnp.zeros((8 * count, eighth), F32)
    for k in range(CHUNKS):
        hit = select(here & (aimed == (base + PAIR * k).astype(F32)))
        total += dot(hit, back[k, :, :, :eighth].reshape(slots, eighth))
    for q in range(8):
        out_tokens[:, q * eighth:(q + 1) * eighth] = (
            total[q * count:(q + 1) * count].astype(BF16)
        )
    copies.append(pltpu.make_async_copy(out_tokens, tokens_out, sem.at[4]))
    copies[-1].start()
    col = iota((count, slots), 1)
    inner = col % BLOCK
    wanted = (col // BLOCK) * CAPACITY + inner
    hit = (inner < CAPACITY) & (jnp.broadcast_to(target, (count, slots)) == wanted.astype(F32))
    total = dot(select(hit), back[CHUNKS - 1, :, :, eighth:].reshape(slots, LANES))
    eye = iota((count, count), 0) == iota((count, count), 1)
    spread = jnp.where(eye, jnp.broadcast_to(total[:, :1], (count, count)), 0.0)
    out_prob[...] = jnp.sum(spread, axis=0, keepdims=True).astype(BF16)
    for copy in copies:
        copy.wait()


def per_device(tokens, grad_out, gate_prob, expert_ids, w_gate, w_up, w_down):
    count, width = tokens.shape
    units = w_gate.shape[2]
    quarter, eighth, half = width // 4, width // 8, width // 2
    vmem = pl.BlockSpec(memory_space=pltpu.VMEM)
    anywhere = pl.BlockSpec(memory_space=pl.ANY)
    rows = CHUNKS * ROWS
    dma = pltpu.SemaphoreType.DMA
    ids = expert_ids.reshape(1, count)
    back, *made = pl.pallas_call(
        kernel,
        out_shape=(
            pltpu.VMEM((CHUNKS, OWNERS, BLOCK, eighth + LANES), BF16),
            pltpu.VMEM(w_gate.shape, BF16),
            pltpu.VMEM(w_up.shape, BF16),
            pltpu.VMEM(w_down.shape, BF16),
        ),
        in_specs=[anywhere] * 2 + [vmem] * 2 + [anywhere] * 3,
        out_specs=[vmem] * 4,
        scratch_shapes=[
            pltpu.VMEM((8 * count, quarter + LANES), BF16),
            pltpu.VMEM((CHUNKS, OWNERS, BLOCK, quarter + LANES), BF16),
            pltpu.VMEM((CHUNKS, OWNERS, BLOCK, quarter + LANES), BF16),
            pltpu.VMEM((CHUNKS, SIDE, SIDE, BLOCK, width + LANES), BF16),
            pltpu.VMEM((CHUNKS, SIDE, SIDE, BLOCK, width), BF16),
            pltpu.VMEM((CHUNKS, SIDE, SIDE, BLOCK, width), BF16),
            pltpu.VMEM((CHUNKS, 4, 2, SIDE, BLOCK, eighth), BF16),
            pltpu.VMEM((CHUNKS, 4, 2, SIDE, BLOCK, quarter), BF16),
            pltpu.VMEM((CHUNKS, 4, 2, BLOCK, eighth), BF16),
            pltpu.VMEM((CHUNKS, 4, 2, BLOCK, quarter), BF16),
            pltpu.VMEM((4, BLOCK, quarter), BF16),
            pltpu.VMEM((8 * BLOCK, eighth + LANES), BF16),
            pltpu.VMEM((CHUNKS, OWNERS, BLOCK, eighth + LANES), BF16),
            pltpu.VMEM((ROWS, 3 * units), F32),
            pltpu.VMEM((rows, 2 * units), BF16),
            pltpu.VMEM((rows, units), BF16),
            pltpu.VMEM((SIDE, SIDE, 8, LANES), F32),
            pltpu.VMEM((SIDE * SIDE, 8, LANES), F32),
            dma((8,)),
            dma((3,)),
            dma((CHUNKS, OWNERS)),
            dma((CHUNKS, OWNERS)),
            dma((CHUNKS, 2, 20)),
            dma((CHUNKS, 2, 20)),
            dma((CHUNKS, 4, 8)),
            dma((CHUNKS, 4, 8)),
            dma((SIDE * SIDE,)),
            dma((SIDE * SIDE,)),
            dma((CHUNKS, OWNERS)),
            dma((CHUNKS, OWNERS)),
        ],
        compiler_params=pltpu.CompilerParams(
            collective_id=0, has_side_effects=True, vmem_limit_bytes=46 * 2**20
        ),
    )(tokens, grad_out, gate_prob[None], ids, w_gate, w_up, w_down)
    grad_tokens, grad_prob, *grads = pl.pallas_call(
        finish,
        out_shape=(
            jax.ShapeDtypeStruct((count, width), BF16),
            jax.ShapeDtypeStruct((1, count), BF16),
            *(jax.ShapeDtypeStruct(grad.shape, BF16) for grad in made),
        ),
        in_specs=[vmem] + [anywhere] * 4,
        out_specs=[anywhere, vmem] + [anywhere] * 3,
        scratch_shapes=[
            pltpu.VMEM(back.shape, BF16), pltpu.VMEM((count, width), BF16), dma((5,))
        ],
        compiler_params=pltpu.CompilerParams(vmem_limit_bytes=6 * 2**20),
    )(ids, back, *made)
    return (grad_tokens, grad_prob[0], *grads)


def solution(mesh):
    in_specs = (
        P(("ctx", "tp"), None),
        P(("ctx", "tp"), None),
        P(("ctx", "tp")),
        P(("ctx", "tp"), None),
        P("ctx", None, "tp"),
        P("ctx", None, "tp"),
        P("ctx", "tp", None),
    )
    out_specs = (
        P(("ctx", "tp"), None),
        P(("ctx", "tp")),
        P("ctx", None, "tp"),
        P("ctx", None, "tp"),
        P("ctx", "tp", None),
    )
    return jax.shard_map(
        per_device, mesh=mesh, in_specs=in_specs, out_specs=out_specs, check_vma=False
    )
```

```python
import jax
import jax.numpy as jnp
from jax import lax
from jax.experimental import pallas as pl
from jax.experimental.pallas import tpu as pltpu
from jax.sharding import PartitionSpec as P

F32 = jnp.float32
BF16 = jnp.bfloat16
SIDE = 4
OWNERS = 8
PAIR = 2
CHUNKS = 3
CAPACITY = PAIR * CHUNKS
BLOCK = OWNERS * PAIR
ROWS = SIDE * SIDE * BLOCK
LANES = 128


def dot(a, b):
    return jnp.dot(a, b, preferred_element_type=F32)


def dot_nt(a, b):
    return lax.dot_general(a, b, (((1,), (1,)), ((), ())), preferred_element_type=F32)


def dot_tn(a, b):
    return lax.dot_general(a, b, (((0,), (0,)), ((), ())), preferred_element_type=F32)


def iota(shape, dim):
    return lax.broadcasted_iota(jnp.int32, shape, dim)


def select(mask):
    return jnp.where(mask, 1.0, 0.0).astype(BF16)


def column(line):
    count = line.shape[1]
    eye = iota((count, count), 0) == iota((count, count), 1)
    spread = jnp.broadcast_to(line[...].astype(F32), (count, count))
    return jnp.sum(jnp.where(eye, spread, 0.0), axis=1, keepdims=True)


def targets(ids):
    count = ids.shape[1]
    chosen = column(ids)
    onehot = jnp.where(chosen == iota((count, LANES), 1).astype(F32), 1.0, 0.0)
    lower = select(iota((count, count), 0) >= iota((count, count), 1))
    ranks = dot(lower, onehot.astype(BF16))
    slot = jnp.sum(ranks * onehot, axis=1, keepdims=True) - 1.0
    return chosen * CAPACITY + slot


def kernel(
    tokens, grads, prob, ids, wg_in, wu_in, wd_in,
    rrcv, out_wg, out_wu, out_wd,
    stk, snd, rcv, ga, gb, part, s1, s2, t1, t2, t3, fin, rsnd,
    acc, dd, wei, pps, ppr,
    i_sem, w_sem, p1_send, p1_recv, ag_send, ag_recv, rs_send, rs_recv,
    pp_send, pp_recv, rt_send, rt_recv,
):
    count, width = tokens.shape
    wg, wu, wd = out_wg.at[0], out_wu.at[0], out_wd.at[0]
    units = wg.shape[1]
    quarter, eighth, half = width // 4, width // 8, width // 2
    c = lax.axis_index("ctx")
    t = lax.axis_index("tp")
    x, z = t // SIDE, t % SIDE

    def at_xz(xd, zd):
        return {"ctx": c, "tp": xd * SIDE + zd}

    def step(p, by):
        return (p + by + SIDE) % SIDE

    barrier = pltpu.get_barrier_semaphore()
    for dc in range(1, OWNERS):
        pl.semaphore_signal(
            barrier, inc=1, device_id={"ctx": (c + dc) % OWNERS, "tp": t},
            device_id_type=pl.DeviceIdType.MESH,
        )
    for d in range(1, SIDE * SIDE):
        pl.semaphore_signal(
            barrier, inc=1, device_id=at_xz(step(x, d // SIDE), step(z, d % SIDE)),
            device_id_type=pl.DeviceIdType.MESH,
        )

    stacking = [
        pltpu.make_async_copy(
            src.at[:, q * quarter:(q + 1) * quarter],
            stk.at[pl.ds((2 * q + n) * count, count), pl.ds(0, quarter)],
            i_sem.at[2 * q + n],
        )
        for q in range(4)
        for n, src in enumerate((tokens, grads))
    ]
    for copy in stacking:
        copy.start()
    loads = [
        pltpu.make_async_copy(src, dst, w_sem.at[i])
        for i, (src, dst) in enumerate(((wg_in.at[0], wg), (wu_in.at[0], wu), (wd_in.at[0], wd)))
    ]
    for copy in loads:
        copy.start()

    sent = []

    def drain(keep=0):
        while len(sent) > keep:
            sent.pop(0).wait_send()

    def send(src, dst, send_sem, recv_sem, device):
        copy = pltpu.make_async_remote_copy(
            src_ref=src, dst_ref=dst, send_sem=send_sem, recv_sem=recv_sem,
            device_id=device, device_id_type=pl.DeviceIdType.MESH,
        )
        copy.start()
        sent.append(copy)
        return copy

    deck = 8 * count

    target = targets(ids)
    target_row = jnp.sum(
        jnp.where(
            iota((count, deck), 0) == iota((count, deck), 1) % count,
            jnp.broadcast_to(target, (count, deck)), 0.0,
        ),
        axis=0, keepdims=True,
    )
    stk[:, quarter:] = jnp.zeros((deck, LANES), BF16)
    stk[:count, quarter:] = jnp.broadcast_to(column(prob), (count, LANES)).astype(BF16)
    slots = OWNERS * BLOCK

    def build(k):
        row, col = iota((slots, deck), 0), iota((slots, deck), 1)
        inner = row % BLOCK
        want = (row // BLOCK) * CAPACITY + PAIR * k + inner % PAIR
        hit = jnp.broadcast_to(target_row, (slots, deck)) == want.astype(F32)
        pick = select(hit & (inner // PAIR == col // count))
        snd[k] = dot(pick, stk[...]).astype(BF16).reshape(OWNERS, BLOCK, quarter + LANES)

    p1 = {}

    def disperse(k):
        for dc in range(1, OWNERS):
            to = (c + dc) % OWNERS
            p1[k, dc] = send(
                snd.at[k, to], rcv.at[k, c], p1_send.at[k, dc], p1_recv.at[k, dc],
                {"ctx": to, "tp": t},
            )
        rcv[k, c] = snd[k, c]

    def assemble(k):
        for dc in range(1, OWNERS):
            p1[k, dc].wait_recv()
        row, col = iota((slots, slots), 0), iota((slots, slots), 1)
        one = row % BLOCK
        where = (one // PAIR) * BLOCK + (row // BLOCK) * PAIR + one % PAIR
        got = dot(select(col == where), rcv[k].reshape(slots, quarter + LANES)).astype(BF16)
        for q in range(4):
            cols = slice(q * quarter, (q + 1) * quarter)
            ga[k, z, x, :, cols] = got[2 * q * BLOCK:(2 * q + 1) * BLOCK, :quarter]
            gb[k, z, x, :, cols] = got[(2 * q + 1) * BLOCK:(2 * q + 2) * BLOCK, :quarter]
        ga[k, z, x, :, width:] = got[:BLOCK, quarter:]

    ag = {}
    halves = (
        (pl.ds(0, half), pl.ds(half, half + LANES)),
        (pl.ds(0, half), pl.ds(half, half)),
    )

    def ag_send_one(k, arr, n, ref, device):
        ag[k, arr, n] = send(ref, ref, ag_send.at[k, arr, n], ag_recv.at[k, arr, n], device)

    def near(arr, stage, by):
        along_x = (arr == 0) == (stage == 1)
        return at_xz(step(x, by), z) if along_x else at_xz(x, step(z, by))

    BOTH = ((0, 1), (1, -1))
    AROUND = (0, -1, 1, 2)

    def block(k, arr, first, second, cols=None):
        xd, zd = (step(x, first), step(z, second)) if arr == 0 else (step(x, second), step(z, first))
        buf = (ga, gb)[arr]
        return buf.at[k, zd, xd] if cols is None else buf.at[k, zd, xd, :, cols]

    def across(k, arr, n):
        for side, by in ((0, 1), (1, -1)):
            ag_send_one(k, arr, 4 + 2 * n + side, block(k, arr, AROUND[n], 0), near(arr, 2, by))

    def g1(k):
        for arr in range(2):
            ag_send_one(k, arr, 0, block(k, arr, 0, 0), near(arr, 1, 1))
            ag_send_one(k, arr, 1, block(k, arr, 0, 0), near(arr, 1, -1))
        for arr in range(2):
            across(k, arr, 0)

    def g2(k, arr, side):
        by = BOTH[side][1]
        ag[k, arr, side].wait_recv()
        ag_send_one(k, arr, 2 + side, block(k, arr, -by, 0, halves[arr][side]), near(arr, 1, by))
        across(k, arr, 1 + side)

    def g3(k, arr):
        ag[k, arr, 2].wait_recv()
        ag[k, arr, 3].wait_recv()
        across(k, arr, 3)

    def g4(k, arr, n, side):
        by = BOTH[side][1]
        ag[k, arr, 4 + 2 * n + side].wait_recv()
        ag_send_one(
            k, arr, 12 + 2 * n + side,
            block(k, arr, AROUND[n], -by, halves[arr][side]), near(arr, 2, by),
        )

    def g5(k):
        for arr in range(2):
            for n in range(12, 20):
                ag[k, arr, n].wait_recv()

    deep = quarter
    wide = width // 10

    def products(k, first, last):
        def one(i, fresh):
            at = pl.ds(pl.multiple_of(i * deep, deep), deep)
            rows_in = ga[k, :, :, :, at].reshape(ROWS, deep)
            rows_grad = gb[k, :, :, :, at].reshape(ROWS, deep)
            gu = dot(rows_in, jnp.concatenate([wg[at, :], wu[at, :]], axis=1))
            raw = dot_nt(rows_grad, wd[:, at])
            acc[:, :2 * units] = gu if fresh else acc[:, :2 * units] + gu
            acc[:, 2 * units:] = raw if fresh else acc[:, 2 * units:] + raw

        if first == 0:
            one(0, True)
            first = 1

        @pl.loop(first, last)
        def _(i):
            one(i, False)

    def forward(k):
        part_rows = 2 * LANES // 4

        @pl.loop(0, ROWS // part_rows)
        def _(i):
            at = pl.ds(pl.multiple_of(i * part_rows, part_rows), part_rows)
            keep = pl.ds(pl.multiple_of(k * ROWS + i * part_rows, part_rows), part_rows)
            g, u, raw = acc[at, :units], acc[at, units:2 * units], acc[at, 2 * units:]
            sig = jax.nn.sigmoid(g)
            act = g * sig
            hidden = act * u
            probs = ga[k, i, :, :, width:].reshape(part_rows, LANES).astype(F32)[:, :1]
            wei[keep, :] = (probs * hidden).astype(BF16)
            dh = probs * raw
            dd[keep, :units] = (dh * u * sig * (1.0 + g * (1.0 - sig))).astype(BF16)
            dd[keep, units:] = (dh * act).astype(BF16)
            sums = jnp.broadcast_to(
                jnp.sum(hidden * raw, axis=1, keepdims=True), (part_rows, LANES)
            )
            spot = iota((part_rows, LANES), 1) == k * BLOCK + iota((part_rows, LANES), 0) % BLOCK
            lanes = jnp.sum(
                jnp.where(spot, sums, 0.0).reshape(SIDE, BLOCK, LANES), axis=1, keepdims=True
            )
            lanes = jnp.broadcast_to(lanes, (SIDE, 8, LANES))
            pps[i] = lanes if k == 0 else pps[i] + lanes

    def backward(k, p, h):
        rows = dd[k * ROWS:(k + 1) * ROWS, :]

        if True:
            at = pl.ds(h * half + p * quarter, quarter)
            value = dot_nt(rows, jnp.concatenate([wg[at, :], wu[at, :]], axis=1))
            part[k, :, :, :, at] = value.astype(BF16).reshape(SIDE, SIDE, BLOCK, quarter)

    rs = {}

    def rs_send_one(k, h, p, n, src, dst, device):
        m = 2 * h + p
        rs[k, m, n] = send(src, dst, rs_send.at[k, m, n], rs_recv.at[k, m, n], device)

    def cols_of(h, p, side=None):
        at = h * half + p * quarter
        return slice(at, at + quarter) if side is None else slice(at + side * eighth, at + (side + 1) * eighth)

    def group(h, by):
        return (step(z, by), slice(None)) if h == 0 else (slice(None), step(x, by))

    def own(h, by):
        return (z, step(x, by)) if h == 0 else (step(z, by), x)

    def add_into(where, others):
        value = part[where].astype(F32)
        for other in others:
            value += other[...].astype(F32)
        part[where] = value.astype(BF16)

    def r1(k, p, h):
        far = (k,) + group(h, 2) + (slice(None),)
        for side, by in BOTH:
            rs_send_one(k, h, p, side, part.at[far + (cols_of(h, p, side),)],
                        s1.at[k, 2 * h + p, side], near(h, 2, by))

    def r2(k, p, h, side):
        by = BOTH[side][1]
        rs[k, 2 * h + p, side].wait_recv()
        to = (k,) + group(h, by) + (slice(None),)
        add_into(to + (cols_of(h, p, side),), (s1.at[k, 2 * h + p, side],))
        rs_send_one(k, h, p, 2 + side, part.at[to + (cols_of(h, p),)],
                    s2.at[k, 2 * h + p, side], near(h, 2, by))

    def r3(k, p, h):
        m = 2 * h + p
        rs[k, m, 2].wait_recv()
        rs[k, m, 3].wait_recv()
        far = (k,) + own(h, 2) + (slice(None),)
        mine = (k,) + group(h, 0) + (slice(None), cols_of(h, p))
        add_into(mine, (s2.at[k, m, 0], s2.at[k, m, 1]))
        if k == CHUNKS - 1:
            for n, by, dst in ((6, 1, t2.at[k, m, 0]), (7, -1, t2.at[k, m, 1]), (4, 2, t3.at[m])):
                to = (k,) + own(h, by) + (slice(None), cols_of(h, p))
                rs_send_one(k, h, p, n, part.at[to], dst, near(h, 1, by))
            return
        for side, by in BOTH:
            rs_send_one(k, h, p, 4 + side, part.at[far + (cols_of(h, p, side),)],
                        t1.at[k, m, side], near(h, 1, by))

    def r4(k, p, h, side):
        m = 2 * h + p
        by = BOTH[side][1]
        rs[k, m, 4 + side].wait_recv()
        to = (k,) + own(h, by) + (slice(None),)
        add_into(to + (cols_of(h, p, side),), (t1.at[k, m, side],))
        rs_send_one(k, h, p, 6 + side, part.at[to + (cols_of(h, p),)],
                    t2.at[k, m, side], near(h, 1, by))

    rt = {}

    def r5(k):
        for m in range(4):
            rs[k, m, 6].wait_recv()
            rs[k, m, 7].wait_recv()
            value = part[(k, z, x, slice(None), cols_of(m // 2, m % 2))].astype(F32)
            value += t2[k, m, 0].astype(F32) + t2[k, m, 1].astype(F32)
            if k == CHUNKS - 1:
                rs[k, m, 4].wait_recv()
                value += t3[m].astype(F32)
            for q in range(2):
                at = (2 * m + q) * BLOCK
                fin[at:at + BLOCK, :eighth] = value[:, q * eighth:(q + 1) * eighth].astype(BF16)
        span = pl.ds(0, eighth)
        if k == 0:
            fin[CHUNKS * BLOCK:, eighth:] = jnp.zeros((slots - CHUNKS * BLOCK, LANES), BF16)
        if k == CHUNKS - 1:
            span = pl.ds(0, eighth + LANES)
            for d in range(1, SIDE * SIDE):
                pp[d].wait_recv()
            ppr[0] = pps[z, x]
            summed = jnp.sum(ppr[...], axis=0)[:1]
            held = CHUNKS * BLOCK
            diagonal = iota((held, LANES), 0) == iota((held, LANES), 1)
            column = jnp.sum(
                jnp.where(diagonal, jnp.broadcast_to(summed, (held, LANES)), 0.0),
                axis=1, keepdims=True,
            )
            column = jnp.broadcast_to(column, (held, LANES)).astype(BF16)
            fin[:held, eighth:] = column
        row, col = iota((slots, slots), 0), iota((slots, slots), 1)
        inner = row % BLOCK
        place = (inner // PAIR) * BLOCK + (row // BLOCK) * PAIR + inner % PAIR
        moved = dot(select(col == place), fin[:, span]).astype(BF16)
        rsnd[k, :, :, span] = moved.reshape(OWNERS, BLOCK, moved.shape[1])
        for dc in range(1, OWNERS):
            to = (c + dc) % OWNERS
            rt[k, dc] = send(
                rsnd.at[k, to, :, span], rrcv.at[k, c, :, span],
                rt_send.at[k, dc], rt_recv.at[k, dc], {"ctx": to, "tp": t},
            )
        rrcv[k, c, :, span] = rsnd[k, c, :, span]

    pp = {}

    def probs_out():
        for d in range(1, SIDE * SIDE):
            xd, zd = step(x, d // SIDE), step(z, d % SIDE)
            pp[d] = send(pps.at[zd, xd], ppr.at[d], pp_send.at[d], pp_recv.at[d], at_xz(xd, zd))

    def weight_in(first, last):
        @pl.loop(first, last)
        def _(i):
            at = pl.ds(pl.multiple_of(i * wide, wide), wide)
            rows_in = ga[:, :, :, :, at].reshape(CHUNKS * ROWS, wide)
            value = dot_tn(rows_in, dd[...])
            wg[at, :] = value[:, :units].astype(BF16)
            wu[at, :] = value[:, units:].astype(BF16)

    def weight_down(first, last):
        @pl.loop(first, last)
        def _(i):
            at = pl.ds(pl.multiple_of(i * wide, wide), wide)
            rows_grad = gb[:, :, :, :, at].reshape(CHUNKS * ROWS, wide)
            wd[:, at] = dot_tn(wei[...], rows_grad).astype(BF16)

    for copy in stacking:
        copy.wait()
    build(0)
    pl.semaphore_wait(barrier, OWNERS - 1 + SIDE * SIDE - 1)
    disperse(0)
    build(1)
    build(2)
    assemble(0)
    g1(0)
    disperse(1)
    g2(0,0,0)
    g2(0,0,1)
    g2(0,1,0)
    g2(0,1,1)
    assemble(1)
    g1(1)
    disperse(2)
    g4(0,1,0,0)
    g4(0,1,0,1)
    g4(0,0,0,0)
    g4(0,0,0,1)
    g3(0,0)
    g4(0,0,1,0)
    g4(0,0,1,1)
    g4(0,1,1,0)
    g4(0,1,1,1)
    g4(0,0,2,0)
    g4(0,0,2,1)
    g4(0,1,2,0)
    g4(0,1,2,1)
    g3(0,1)
    g2(1,0,0)
    g2(1,0,1)
    g2(1,1,0)
    g2(1,1,1)
    assemble(2)
    g1(2)
    g4(1,1,0,0)
    g4(1,1,0,1)
    g4(1,0,0,0)
    g4(1,0,0,1)
    g4(0,0,3,0)
    g4(0,0,3,1)
    g4(0,1,3,0)
    g4(0,1,3,1)
    g3(1,0)
    g4(1,0,1,0)
    g4(1,0,1,1)
    g4(1,1,1,0)
    g4(1,1,1,1)
    g4(1,0,2,0)
    g4(1,0,2,1)
    g4(1,1,2,0)
    g4(1,1,2,1)
    g3(1,1)
    g2(2,0,0)
    g2(2,0,1)
    g2(2,1,0)
    g2(2,1,1)
    g4(2,1,0,0)
    g4(2,1,0,1)
    g4(2,0,0,0)
    g4(2,0,0,1)
    g5(0)
    for copy in loads:
        copy.wait()
    products(0,0,3)
    g4(1,0,3,0)
    g4(1,0,3,1)
    products(0,3,4)
    forward(0)
    g4(1,1,3,0)
    g4(1,1,3,1)
    backward(0,0,0)
    backward(0,0,1)
    backward(0,1,0)
    g3(2,0)
    backward(0,1,1)
    g4(2,0,1,0)
    g4(2,0,1,1)
    g4(2,1,1,0)
    g4(2,1,1,1)
    g4(2,0,2,0)
    g4(2,0,2,1)
    g4(2,1,2,0)
    g4(2,1,2,1)
    g3(2,1)
    g5(1)
    r1(0,0,0)
    r1(0,0,1)
    r1(0,1,0)
    r1(0,1,1)
    products(1,0,2)
    g4(2,0,3,0)
    g4(2,0,3,1)
    products(1,2,4)
    g4(2,1,3,0)
    g4(2,1,3,1)
    forward(1)
    backward(1,0,0)
    r2(0,0,1,0)
    r2(0,0,1,1)
    r2(0,0,0,0)
    backward(1,0,1)
    r2(0,1,1,0)
    r2(0,0,0,1)
    r2(0,1,1,1)
    backward(1,1,0)
    r2(0,1,0,0)
    backward(1,1,1)
    r2(0,1,0,1)
    g5(2)
    r1(1,0,0)
    r1(1,0,1)
    r1(1,1,0)
    r1(1,1,1)
    products(2,0,1)
    r3(0,0,1)
    products(2,1,2)
    r3(0,0,0)
    products(2,2,3)
    r3(0,1,1)
    products(2,3,4)
    r3(0,1,0)
    r2(1,0,0,0)
    r2(1,0,1,0)
    r2(1,0,1,1)
    forward(2)
    r4(0,0,0,0)
    r4(0,0,0,1)
    r2(1,0,0,1)
    r2(1,1,0,0)
    r2(1,1,1,0)
    r4(0,0,1,0)
    r2(1,1,1,1)
    r4(0,1,1,0)
    backward(2,0,0)
    r4(0,0,1,1)
    r4(0,1,0,0)
    r4(0,1,0,1)
    r4(0,1,1,1)
    r2(1,1,0,1)
    r1(2,0,0)
    backward(2,0,1)
    r1(2,0,1)
    backward(2,1,0)
    r1(2,1,0)
    backward(2,1,1)
    r1(2,1,1)
    probs_out()
    r3(1,0,1)
    weight_in(0,1)
    r3(1,0,0)
    weight_in(1,3)
    r3(1,1,1)
    weight_in(3,4)
    r5(0)
    r3(1,1,0)
    r2(2,0,0,0)
    r2(2,0,1,0)
    r2(2,0,0,1)
    r2(2,0,1,1)
    r4(1,0,1,0)
    r4(1,0,0,0)
    r2(2,1,0,0)
    r4(1,0,0,1)
    r4(1,1,1,0)
    r2(2,1,1,0)
    r2(2,1,1,1)
    weight_in(4,5)
    r4(1,0,1,1)
    r4(1,1,1,1)
    r4(1,1,0,0)
    r4(1,1,0,1)
    r2(2,1,0,1)
    weight_in(5,9)
    r3(2,0,0)
    r3(2,0,1)
    weight_in(9,10)
    weight_down(0,4)
    r3(2,1,1)
    r3(2,1,0)
    r5(1)
    weight_down(4,10)
    r5(2)

    for k in range(CHUNKS):
        for dc in range(1, OWNERS):
            rt[k, dc].wait_recv()
    drain()


def finish(
    ids, back_in, wg, wu, wd, tokens_out, out_prob, out_wg, out_wu, out_wd,
    back, out_tokens, sem,
):
    copies = [
        pltpu.make_async_copy(src, dst, sem.at[i])
        for i, (src, dst) in enumerate(
            ((back_in, back), (wg, out_wg), (wu, out_wu), (wd, out_wd))
        )
    ]
    for copy in copies:
        copy.start()
    count = ids.shape[1]
    eighth = back.shape[3] - LANES
    slots = OWNERS * BLOCK
    target = targets(ids)
    aimed = jnp.broadcast_to(jnp.concatenate([target] * 8, axis=0), (8 * count, slots))
    row, col = iota((8 * count, slots), 0), iota((8 * count, slots), 1)
    inner = col % BLOCK
    base = (col // BLOCK) * CAPACITY + inner % PAIR
    here = inner // PAIR == row // count
    copies.pop(0).wait()
    total = jnp.zeros((8 * count, eighth), F32)
    for k in range(CHUNKS):
        hit = select(here & (aimed == (base + PAIR * k).astype(F32)))
        total += dot(hit, back[k, :, :, :eighth].reshape(slots, eighth))
    for q in range(8):
        out_tokens[:, q * eighth:(q + 1) * eighth] = (
            total[q * count:(q + 1) * count].astype(BF16)
        )
    copies.append(pltpu.make_async_copy(out_tokens, tokens_out, sem.at[4]))
    copies[-1].start()
    col = iota((count, slots), 1)
    inner = col % BLOCK
    wanted = (col // BLOCK) * CAPACITY + inner
    hit = (inner < CAPACITY) & (jnp.broadcast_to(target, (count, slots)) == wanted.astype(F32))
    total = dot(select(hit), back[CHUNKS - 1, :, :, eighth:].reshape(slots, LANES))
    eye = iota((count, count), 0) == iota((count, count), 1)
    spread = jnp.where(eye, jnp.broadcast_to(total[:, :1], (count, count)), 0.0)
    out_prob[...] = jnp.sum(spread, axis=0, keepdims=True).astype(BF16)
    for copy in copies:
        copy.wait()


def per_device(tokens, grad_out, gate_prob, expert_ids, w_gate, w_up, w_down):
    count, width = tokens.shape
    units = w_gate.shape[2]
    quarter, eighth, half = width // 4, width // 8, width // 2
    vmem = pl.BlockSpec(memory_space=pltpu.VMEM)
    anywhere = pl.BlockSpec(memory_space=pl.ANY)
    rows = CHUNKS * ROWS
    dma = pltpu.SemaphoreType.DMA
    ids = expert_ids.reshape(1, count)
    back, *made = pl.pallas_call(
        kernel,
        out_shape=(
            pltpu.VMEM((CHUNKS, OWNERS, BLOCK, eighth + LANES), BF16),
            pltpu.VMEM(w_gate.shape, BF16),
            pltpu.VMEM(w_up.shape, BF16),
            pltpu.VMEM(w_down.shape, BF16),
        ),
        in_specs=[anywhere] * 2 + [vmem] * 2 + [anywhere] * 3,
        out_specs=[vmem] * 4,
        scratch_shapes=[
            pltpu.VMEM((8 * count, quarter + LANES), BF16),
            pltpu.VMEM((CHUNKS, OWNERS, BLOCK, quarter + LANES), BF16),
            pltpu.VMEM((CHUNKS, OWNERS, BLOCK, quarter + LANES), BF16),
            pltpu.VMEM((CHUNKS, SIDE, SIDE, BLOCK, width + LANES), BF16),
            pltpu.VMEM((CHUNKS, SIDE, SIDE, BLOCK, width), BF16),
            pltpu.VMEM((CHUNKS, SIDE, SIDE, BLOCK, width), BF16),
            pltpu.VMEM((CHUNKS, 4, 2, SIDE, BLOCK, eighth), BF16),
            pltpu.VMEM((CHUNKS, 4, 2, SIDE, BLOCK, quarter), BF16),
            pltpu.VMEM((CHUNKS, 4, 2, BLOCK, eighth), BF16),
            pltpu.VMEM((CHUNKS, 4, 2, BLOCK, quarter), BF16),
            pltpu.VMEM((4, BLOCK, quarter), BF16),
            pltpu.VMEM((8 * BLOCK, eighth + LANES), BF16),
            pltpu.VMEM((CHUNKS, OWNERS, BLOCK, eighth + LANES), BF16),
            pltpu.VMEM((ROWS, 3 * units), F32),
            pltpu.VMEM((rows, 2 * units), BF16),
            pltpu.VMEM((rows, units), BF16),
            pltpu.VMEM((SIDE, SIDE, 8, LANES), F32),
            pltpu.VMEM((SIDE * SIDE, 8, LANES), F32),
            dma((8,)),
            dma((3,)),
            dma((CHUNKS, OWNERS)),
            dma((CHUNKS, OWNERS)),
            dma((CHUNKS, 2, 20)),
            dma((CHUNKS, 2, 20)),
            dma((CHUNKS, 4, 8)),
            dma((CHUNKS, 4, 8)),
            dma((SIDE * SIDE,)),
            dma((SIDE * SIDE,)),
            dma((CHUNKS, OWNERS)),
            dma((CHUNKS, OWNERS)),
        ],
        compiler_params=pltpu.CompilerParams(
            collective_id=0, has_side_effects=True, vmem_limit_bytes=46 * 2**20
        ),
    )(tokens, grad_out, gate_prob[None], ids, w_gate, w_up, w_down)
    grad_tokens, grad_prob, *grads = pl.pallas_call(
        finish,
        out_shape=(
            jax.ShapeDtypeStruct((count, width), BF16),
            jax.ShapeDtypeStruct((1, count), BF16),
            *(jax.ShapeDtypeStruct(grad.shape, BF16) for grad in made),
        ),
        in_specs=[vmem] + [anywhere] * 4,
        out_specs=[anywhere, vmem] + [anywhere] * 3,
        scratch_shapes=[
            pltpu.VMEM(back.shape, BF16), pltpu.VMEM((count, width), BF16), dma((5,))
        ],
        compiler_params=pltpu.CompilerParams(vmem_limit_bytes=6 * 2**20),
    )(ids, back, *made)
    return (grad_tokens, grad_prob[0], *grads)


def solution(mesh):
    in_specs = (
        P(("ctx", "tp"), None),
        P(("ctx", "tp"), None),
        P(("ctx", "tp")),
        P(("ctx", "tp"), None),
        P("ctx", None, "tp"),
        P("ctx", None, "tp"),
        P("ctx", "tp", None),
    )
    out_specs = (
        P(("ctx", "tp"), None),
        P(("ctx", "tp")),
        P("ctx", None, "tp"),
        P("ctx", None, "tp"),
        P("ctx", "tp", None),
    )
    return jax.shard_map(
        per_device, mesh=mesh, in_specs=in_specs, out_specs=out_specs, check_vma=False
    )
```
